256 devices in a mesh: blk: 32 (over z, x_lo, core), grp: 8 (over x_hi, y).
Axes of the slice: x: 4 (x_hi: 2, x_lo: 2; x = x_hi * 2 + x_lo), y: 4, z: 8, core: 2. Of those that a mesh axis runs over, the one named last changes fastest.
Arguments:
- image_embed: bfloat16 [32768, 1152], P(('blk', 'grp')), may hold values from -0.1796875 to 0.1796875
- text_embed: bfloat16 [32768, 1152], P(('blk', 'grp')), may hold values from -0.1796875 to 0.1796875
- log_scale: float32 [1], replicated, may hold values from 1.6 to 2.6
- bias: float32 [1], replicated, may hold values from -4 to -1
Outputs:
- grad_image: float32 [32768, 1152], P(('blk', 'grp'))
- grad_text: float32 [32768, 1152], P(('blk', 'grp'))
- pair_loss: float32 [], replicated
- grad_log_scale: float32 [], replicated
- grad_bias: float32 [], replicated
The draws below stay inside these ranges and needn't reach their ends.
All inputs are finite; a program needn't handle non-finite values.
Results may differ from the reference program's by a relative error of at most 0.0004.
The reference program's roundings to bfloat16 on the way count: a program that leaves them out, or rounds other values in their place, can miss the bound.
Values may be sent and summed in bfloat16 or wider, within the bound.
A program may use at most 128 MiB of HBM per device.

```python
import jax
import jax.numpy as jnp
from jax import lax

D = 1152
ROWS_DEV = 128
STEPS = 4
BATCH = 32768
N_BLK = 32
N_GRP = 8


def levels(key, shape, cuts, least, top_value):
    def one(dim, blocks):
        steps = jax.random.uniform(jax.random.fold_in(jax.random.fold_in(key, 6), dim), (blocks,), jnp.float32, least / len(cuts), top_value / len(cuts))
        return jnp.repeat(jnp.exp(steps), shape[dim] // blocks).reshape((-1,) + (1,) * (len(shape) - dim - 1))

    factor_of = one(*cuts[0])
    for cut in cuts[1:]:
        factor_of = factor_of * one(*cut)
    return factor_of


def gaussian(own_key, extent, spread, limit, split=(), kind=jnp.bfloat16):
    level = levels(own_key, extent, split, -0.22, 0.18) if split else 1.0
    drawn = jax.random.normal(own_key, extent, jnp.float32) * spread * level
    return jnp.minimum(jnp.maximum(drawn, -limit), limit).astype(kind)


def setup_inputs(seed: int = 0) -> dict:
    streams_of = jax.random.split(jax.random.key(seed), 5)
    return {
        "image_embed": gaussian(streams_of[0], (BATCH, D), 0.03, 0.1796875, ((0, 256),)),
        "text_embed": gaussian(streams_of[1], (BATCH, D), 0.03, 0.1796875, ((0, 256),)),
        "log_scale": jnp.clip(jax.random.uniform(streams_of[2], (1,), jnp.float32, 1.6, 2.6), 1.6, 2.6),
        "bias": jnp.clip(jax.random.uniform(streams_of[3], (1,), jnp.float32, -4.0, -1.0), -4.0, -1.0),
    }


def unit_rows(embed):
    wide = embed.astype(jnp.float32)
    inverse = lax.rsqrt(lax.optimization_barrier(jnp.sum(wide * wide, axis=1, keepdims=True)) + 1e-06)
    return (wide * inverse, inverse)

def reference(image_embed, text_embed, log_scale, bias):
    width = image_embed.shape[1]
    block = N_GRP * ROWS_DEV
    image_unit, image_inv = unit_rows(image_embed)
    text_unit, text_inv = unit_rows(text_embed)
    image_low = image_unit.astype(jnp.bfloat16).reshape(N_BLK, block, width)
    text_low = text_unit.astype(jnp.bfloat16).reshape(N_BLK, block, width)
    scale = jnp.exp(log_scale[0])
    offset = bias[0]
    within = jnp.arange(block, dtype=jnp.int32)
    places = jnp.arange(N_BLK, dtype=jnp.int32)
    image_back = jnp.zeros((N_BLK, block, width), jnp.float32)
    text_back = jnp.zeros((N_BLK, block, width), jnp.float32)
    loss_sum = jnp.float32(0.0)
    scale_sum = jnp.float32(0.0)
    bias_sum = jnp.float32(0.0)
    for step in range(STEPS):
        rolled = jnp.roll(text_low, step, axis=0)

        def one_block(items):
            images, texts, place = items
            anchor = (place - step) % N_BLK
            row_ids = place * block + within
            col_ids = anchor * block + within
            logits = jnp.dot(images, texts.T, preferred_element_type=jnp.float32)
            label = jnp.where(row_ids[:, None] == col_ids[None, :], 1.0, -1.0).astype(jnp.float32)
            score = scale * logits + offset
            loss = jnp.sum(jax.nn.softplus(-label * score))
            slope = -label * jax.nn.sigmoid(-label * score)
            dscale = jnp.sum(slope * logits) * scale
            dbias = jnp.sum(slope)
            weights = (scale * slope).astype(jnp.bfloat16)
            dimage = jnp.dot(weights, texts, preferred_element_type=jnp.float32)
            dtext = jnp.dot(weights.T, images, preferred_element_type=jnp.float32)
            return (dimage, dtext, loss, dscale, dbias)
        dimage, dtext, losses, dscales, dbiases = lax.map(one_block, (image_low, rolled, places))
        image_back = image_back + dimage
        text_back = text_back + jnp.roll(dtext, -step, axis=0)
        loss_sum = loss_sum + jnp.sum(losses)
        scale_sum = scale_sum + jnp.sum(dscales)
        bias_sum = bias_sum + jnp.sum(dbiases)
    image_back = image_back.reshape(-1, width)
    text_back = text_back.reshape(-1, width)
    grad_image = image_inv * (image_back - image_unit * lax.optimization_barrier(jnp.sum(image_unit * image_back, axis=1, keepdims=True)))
    grad_text = text_inv * (text_back - text_unit * lax.optimization_barrier(jnp.sum(text_unit * text_back, axis=1, keepdims=True)))
    pairs = float(N_BLK * block * STEPS * block)
    return (grad_image, grad_text, loss_sum / pairs, scale_sum / pairs, bias_sum / pairs)
```

```python
import functools

import jax
import jax.numpy as jnp
from jax import lax
from jax.experimental import pallas as pl
from jax.experimental.pallas import tpu as pltpu
from jax.sharding import PartitionSpec as P

MESH = pl.DeviceIdType.MESH
STEPS = 4
NT = (((1,), (1,)), ((), ()))
TN = (((0,), (0,)), ((), ()))
NN = (((1,), (0,)), ((), ()))


def normalize(embed):
    wide = embed.astype(jnp.float32)
    inverse = lax.rsqrt(jnp.sum(wide * wide, axis=1, keepdims=True) + 1e-06)
    return wide * inverse, inverse


def finish(embed, back):
    unit, inverse = normalize(embed)
    return inverse * (back - unit * jnp.sum(unit * back, axis=1, keepdims=True))


def dot(a, b, dims):
    return lax.dot_general(a, b, dims, preferred_element_type=jnp.float32)


def kernel(
    n_blk, n_grp,
    scale_ref, bias_ref, image_ref, text_ref,
    grad_image_ref, grad_text_ref, sums_ref,
    images, texts, own_text, scores, weights, text_part, image_part, image_other,
    core_in, image_in, text_in, acc, sums_in,
    image_send, image_recv, share_send, share_recv, text_send, text_recv,
    tgrad_send, tgrad_recv, core_send, core_recv, igrad_send, igrad_recv, sum_send, sum_recv,
):
    rows = image_ref.shape[0]
    p = lax.axis_index("blk")
    g = lax.axis_index("grp")
    c = lax.rem(p, 2)
    base = p - c
    h = g // 4
    y = lax.rem(g, 4)
    sibling = (base + 1 - c, g)

    def ring(blk):
        return lax.rem(blk + n_blk, n_blk)

    def along_y(d):
        return (p, h * 4 + lax.rem(y + d + 4, 4))

    def user(m, hh):
        return (ring(base + 2 * m + h), hh * 4 + y)

    def owner(s):
        return (ring(base - 3 + s), c * 4 + y)

    def each_user(action):
        for m in range(3):
            for hh in range(2):
                here = (c == h) & (h == hh) if m == 0 else False
                there = m < 2 + c
                if m == 0:
                    pl.when(jnp.logical_not(here))(functools.partial(action, m, hh))
                else:
                    pl.when(there)(functools.partial(action, m, hh))

    def each_owner(action):
        for s in range(5):
            if s < 3:
                action(s)
            else:
                mine = (c == h) & (c == s - 3)
                pl.when(jnp.logical_not(mine))(functools.partial(action, s))

    barrier = pltpu.get_barrier_semaphore()

    def greet(device):
        pl.semaphore_signal(barrier, inc=1, device_id=device, device_id_type=MESH)

    for d in (1, 2, 3):
        greet(along_y(d))
    greet(sibling)
    each_user(lambda m, hh: greet(user(m, hh)))
    each_owner(lambda s: greet(owner(s)))
    rounds = [("blk", 1 << r) for r in range(5)] + [("grp", 1 << r) for r in range(3)]

    def partner(r):
        axis, bit = rounds[r]
        if axis == "blk":
            flip = lax.rem(p // bit, 2)
            return (p + bit - 2 * bit * flip, g)
        flip = lax.rem(g // bit, 2)
        return (p, g + bit - 2 * bit * flip)

    for r in range(8):
        greet(partner(r))

    own_low = normalize(image_ref[...])[0].astype(jnp.bfloat16)
    images[c, 0] = own_low
    own_text[...] = normalize(text_ref[...])[0].astype(jnp.bfloat16)
    acc[...] = jnp.zeros_like(acc)

    mine = (c == h).astype(jnp.int32)
    pl.semaphore_wait(barrier, 3 + 1 + 8 + 5 - mine + 2 * (2 + c) - mine)

    def remote(src, dst, send, recv, device):
        return pltpu.make_async_remote_copy(
            src_ref=src, dst_ref=dst, send_sem=send, recv_sem=recv, device_id=device, device_id_type=MESH
        )

    def text_copy(m, hh):
        slot = 3 + c - 2 * m if m < 2 else 0
        return remote(own_text, texts.at[slot], text_send.at[m, hh], text_recv.at[slot], user(m, hh))

    def text_arrival(s):
        return remote(own_text, texts.at[s], text_send.at[0, 0], text_recv.at[s], sibling)

    def image_copy(d):
        slot = (4 - d) % 4
        return remote(images.at[c, 0], images.at[c, slot], image_send.at[d], image_recv.at[slot], along_y(d))

    def share(slot):
        return remote(images.at[c, slot], images.at[c, slot], share_send.at[slot], share_recv.at[slot], sibling)

    for d in (1, 3, 2):
        image_copy(d).start()
    share(0).start()
    each_user(lambda m, hh: text_copy(m, hh).start())

    @pl.when(c == h)
    def _():
        texts[3 + c] = own_text[...]

    for slot in (1, 3, 2):
        image_copy(4 - slot).wait_recv()
        share(slot).start()
    for slot in (0, 1, 3, 2):
        remote(images.at[c, slot], images.at[1 - c, slot], share_send.at[slot], share_recv.at[slot], sibling).wait_recv()

    scale = jnp.exp(scale_ref[0])
    offset = bias_ref[0]
    eye = lax.broadcasted_iota(jnp.int32, (rows, rows), 0) == lax.broadcasted_iota(jnp.int32, (rows, rows), 1)

    def logistic(score):
        small = jnp.exp(-jnp.abs(score))
        whole = 1.0 + small
        inverse = 1.0 / whole
        loss = jnp.maximum(score, 0.0) + (jnp.log(whole) + (small - (whole - 1.0)) * inverse)
        return loss, jnp.where(score >= 0.0, 1.0, small) * inverse

    def tile(s, b, yy, paired):
        logits = scores[:, pl.ds(pl.multiple_of(yy * rows, rows), rows)]
        score = scale * logits + offset
        if paired is None:
            loss, slope = logistic(score)
        else:
            match = eye & paired
            loss, slope = logistic(jnp.where(match, -score, score))
            slope = jnp.where(match, -slope, slope)
        weights[s, b, yy] = (scale * slope).astype(jnp.bfloat16)
        acc[0] += loss.reshape(-1, 8, rows).sum(axis=0)
        acc[1] += (slope * logits).reshape(-1, 8, rows).sum(axis=0)
        acc[2] += slope.reshape(-1, 8, rows).sum(axis=0)

    width = image_ref.shape[1]

    def half(s, b, add):
        block = images[b].reshape(4 * rows, width)
        scores[...] = dot(texts[s], block, NT)
        tile(s, b, 0, (c == h) & (s == 3 + b))

        def body(yy, carry):
            tile(s, b, yy, None)
            return carry

        lax.fori_loop(1, 4, body, 0)
        part = sum(
            dot(weights[s, b, yy], images[b, yy], NN) for yy in range(4)
        )
        if add:
            text_part[s] += part
        else:
            text_part[s] = part

    def tgrad_copy(s):
        m = (4 + c - s) // 2 if isinstance(s, int) else (4 + c - s) // 2
        return m

    def send_part(s):
        m = {0: 2, 1: 1, 2: 1, 3: 0, 4: 0}[s]
        return remote(text_part.at[s], text_in.at[m, h], tgrad_send.at[s], tgrad_recv.at[m, h], owner(s))

    def start_part(s):
        if s < 3:
            send_part(s).start()
        else:
            mine = (c == h) & (c == s - 3)

            @pl.when(jnp.logical_not(mine))
            def _():
                send_part(s).start()

    for s in (3, 4, 2, 1, 0):
        if s >= 3:
            mine = (c == h) & (c == s - 3)
            pl.when(jnp.logical_not(mine))(lambda s=s: text_arrival(s).wait_recv())
        else:
            text_arrival(s).wait_recv()
        if s < 4:
            half(s, 0, False)
        if s > 0:
            half(s, 1, s < 4)
        start_part(s)

    def image_sum(b, yy):
        lhs = weights[pl.ds(b, 4), b, yy].reshape(4 * rows, rows)
        rhs = texts[pl.ds(b, 4)].reshape(4 * rows, width)
        return dot(lhs, rhs, TN)

    def core_copy(slot):
        return remote(image_other.at[slot], core_in.at[slot], core_send.at[slot], core_recv.at[slot], sibling)

    def igrad_copy(slot):
        return remote(image_part.at[slot], image_in.at[4 - slot], igrad_send.at[slot], igrad_recv.at[4 - slot], along_y(slot))

    for slot in (2, 1, 3, 0):
        image_other[slot] = image_sum(1 - c, slot)
        core_copy(slot).start()
    for slot in (2, 1, 3, 0):
        image_part[slot] = image_sum(c, slot)
        core_copy(slot).wait_recv()
        image_part[slot] += core_in[slot]
        if slot:
            igrad_copy(slot).start()

    sums_in[8, 0] = jnp.sum(acc[0], axis=0, keepdims=True)
    sums_in[8, 1] = jnp.sum(acc[1], axis=0, keepdims=True)
    sums_in[8, 2] = jnp.sum(acc[2], axis=0, keepdims=True)
    for r in range(8):
        copy = remote(sums_in.at[8 + r], sums_in.at[r], sum_send.at[r], sum_recv.at[r], partner(r))
        copy.start()
        copy.wait_recv()
        sums_in[9 + r] = sums_in[8 + r] + sums_in[r]
    total = jnp.sum(sums_in[16], axis=-1, keepdims=True)
    pairs = float(n_blk * n_grp * rows * STEPS * n_grp * rows)
    sums_ref[0:1, :] = jnp.broadcast_to(total[0] / pairs, (1, 128))
    sums_ref[1:2, :] = jnp.broadcast_to(total[1] * scale / pairs, (1, 128))
    sums_ref[2:3, :] = jnp.broadcast_to(total[2] / pairs, (1, 128))

    text_back = jnp.where((c == h), 1.0, 0.0)
    del text_back

    def tgrad_arrival(m, hh):
        remote(text_part.at[0], text_in.at[m, hh], tgrad_send.at[0], tgrad_recv.at[m, hh], sibling).wait_recv()

    each_user(tgrad_arrival)

    @pl.when(c == h)
    def _():
        text_in[0, h] = text_part[3 + c]

    @pl.when(c == 0)
    def _():
        text_in[2, 0] = jnp.zeros_like(text_in[2, 0])
        text_in[2, 1] = jnp.zeros_like(text_in[2, 1])

    text_back = text_in[0, 0] + text_in[0, 1] + text_in[1, 0] + text_in[1, 1] + text_in[2, 0] + text_in[2, 1]
    grad_text_ref[...] = finish(text_ref[...], text_back)

    for slot in (1, 3, 2):
        igrad_copy(4 - slot).wait_recv()
    image_back = image_part[0] + image_in[1] + image_in[2] + image_in[3]
    grad_image_ref[...] = finish(image_ref[...], image_back)

    for d in (1, 2, 3):
        image_copy(d).wait_send()
        igrad_copy(d).wait_send()
    for slot in range(4):
        share(slot).wait_send()
        core_copy(slot).wait_send()
    each_user(lambda m, hh: text_copy(m, hh).wait_send())
    each_owner(lambda s: send_part(s).wait_send())
    for r in range(8):
        remote(sums_in.at[8 + r], sums_in.at[r], sum_send.at[r], sum_recv.at[r], partner(r)).wait_send()


def local(n_blk, n_grp, image_embed, text_embed, log_scale, bias):
    rows, width = image_embed.shape
    low, wide = jnp.bfloat16, jnp.float32
    dma = pltpu.SemaphoreType.DMA
    vmem = pl.BlockSpec(memory_space=pltpu.VMEM)
    smem = pl.BlockSpec(memory_space=pltpu.SMEM)
    out = jax.ShapeDtypeStruct((rows, width), wide)
    pairs = n_grp * rows * STEPS * rows
    grad_image, grad_text, sums = pl.pallas_call(
        functools.partial(kernel, n_blk, n_grp),
        out_shape=(out, out, jax.ShapeDtypeStruct((8, 128), wide)),
        in_specs=[smem, smem, vmem, vmem],
        out_specs=(vmem, vmem, vmem),
        scratch_shapes=[
            pltpu.VMEM((2, 4, rows, width), low),
            pltpu.VMEM((5, rows, width), low),
            pltpu.VMEM((rows, width), low),
            pltpu.VMEM((rows, 4 * rows), wide),
            pltpu.VMEM((5, 2, 4, rows, rows), low),
            pltpu.VMEM((5, rows, width), wide),
            pltpu.VMEM((4, rows, width), wide),
            pltpu.VMEM((4, rows, width), wide),
            pltpu.VMEM((4, rows, width), wide),
            pltpu.VMEM((4, rows, width), wide),
            pltpu.VMEM((3, 2, rows, width), wide),
            pltpu.VMEM((3, 8, 128), wide),
            pltpu.VMEM((17, 3, 1, 128), wide),
            dma((4,)), dma((4,)), dma((4,)), dma((4,)), dma((3, 2)), dma((5,)),
            dma((5,)), dma((3, 2)), dma((4,)), dma((4,)), dma((4,)), dma((4,)), dma((8,)), dma((8,)),
        ],
        compiler_params=pltpu.CompilerParams(
            collective_id=0, has_side_effects=True, vmem_limit_bytes=48 << 20
        ),
        cost_estimate=pl.CostEstimate(
            flops=6 * pairs * width, bytes_accessed=12 * rows * width, transcendentals=3 * pairs
        ),
        name="pair_loss",
    )(log_scale, bias, image_embed, text_embed)
    return grad_image, grad_text, sums[0, 0], sums[1, 0], sums[2, 0]


def solution(mesh):
    split = P(("blk", "grp"), None)
    return jax.shard_map(
        functools.partial(local, mesh.shape["blk"], mesh.shape["grp"]),
        mesh=mesh,
        in_specs=(split, split, P(), P()),
        out_specs=(split, split, P(), P(), P()),
        check_vma=False,
    )
```

```python
import functools

import jax
import jax.numpy as jnp
from jax import lax
from jax.experimental import pallas as pl
from jax.experimental.pallas import tpu as pltpu
from jax.sharding import PartitionSpec as P

MESH = pl.DeviceIdType.MESH
STEPS = 4
ROUND = 12582912.0
NT = (((1,), (1,)), ((), ()))
TN = (((0,), (0,)), ((), ()))
NN = (((1,), (0,)), ((), ()))

ORDER = ((2, 1, 0, 3), (1, 0, 1, 0), (0, 2, 3, 2), (3, 3, 2, 4), (4, 4, 4, 1))
PART_Z = ((-1, 0, -1, 0), (0, 0, -1, -1), (-1, 0, 0, 0), (0, 0, 0, 0), (0, 0, 0, 0))
PART_X = ((0, -1, 0, -1), (1, 0, 0, 0), (0, 0, 1, 1), (0, 0, -1, 0), (0, 0, 0, 0))
PART_CORE = ((2, 0, 2, 2), (2, 2, 2, 2), (1, 2, 2, 1), (0, 0, 2, 2), (1, 1, 2, 2))
PART_SLOT = ((1, 4, 0, 2), (1, 0, 1, 0), (6, 0, 1, 5), (3, 3, 0, 0), (3, 3, 0, 0))
SENT = ((1, 1, 1, 1), (1, 0, 1, 1), (1, 0, 1, 1), (2, 2, 1, 0), (3, 3, 0, 0))


def normalize(embed):
    wide = embed.astype(jnp.float32)
    inverse = lax.rsqrt(jnp.sum(wide * wide, axis=1, keepdims=True) + 1e-06)
    return wide * inverse, inverse


def finish(embed, back):
    unit, inverse = normalize(embed)
    return inverse * (back - unit * jnp.sum(unit * back, axis=1, keepdims=True))


def encode(value):
    top = jnp.max(jnp.abs(value), axis=1, keepdims=True)
    step = (jnp.maximum(top, 1e-30) * (1.008 / 16383.0)).astype(jnp.bfloat16).astype(jnp.float32)
    whole = (value * (1.0 / step) + ROUND) - ROUND
    upper = jnp.floor(whole * (1.0 / 128.0))
    lower = whole - 128.0 * upper
    signed = jnp.where(upper >= 0.0, upper + 128.0, upper - 127.0)
    return (signed * jnp.exp2(lower - 71.0)).astype(jnp.bfloat16), step.astype(jnp.bfloat16)


def decode(code, step):
    wide = code.astype(jnp.float32)
    size = jnp.abs(wide)
    power = jnp.floor(jnp.log2(size) + 0.001)
    mantissa = size * jnp.exp2(7.0 - power)
    upper = jnp.where(wide >= 0.0, mantissa - 128.0, 127.0 - mantissa)
    return (upper * 128.0 + (power + 64.0)) * step.astype(jnp.float32)


def dot(a, b, dims):
    return lax.dot_general(a, b, dims, preferred_element_type=jnp.float32)


def kernel(
    n_blk, n_grp,
    scale_ref, bias_ref, image_hbm, text_hbm,
    grad_image_ref, grad_text_ref, sums_ref,
    image_ref, text_ref, load_sem, images, texts, own_text, scores, weights, parts, wires, inbox, late_wires,
    image_part, image_other, core_in, back_wires, relay, image_in, acc, totals,
    ring_send, ring_recv, share_send, share_recv, first_send, hand_send, text_recv,
    part_send, late_send, part_recv, core_send, core_recv, back_send, relay_recv, image_recv,
    total_send, total_recv,
):
    rows, width = image_ref.shape
    chunk = rows // 2
    p = lax.axis_index("blk")
    g = lax.axis_index("grp")
    c = lax.rem(p, 2)
    z = p // 4
    low = lax.rem(p // 2, 2)
    h = g // 4
    y = lax.rem(g, 4)
    x = 2 * h + low
    role = lax.rem(x + 4 - 2 * c, 4)
    depth = n_blk // 4

    def place(dz, dx, core):
        at_x = lax.rem(x + dx + 4, 4)
        at_z = lax.rem(z + dz + depth, depth)
        return (at_z * 4 + lax.rem(at_x, 2) * 2 + core, (at_x // 2) * 4 + y)

    def along_y(d):
        return (p, h * 4 + lax.rem(y + d + 4, 4))

    sibling = (p + 1 - 2 * c, g)

    def pick(row):
        a, b, d, e = row
        return jnp.where(role == 0, a, jnp.where(role == 1, b, jnp.where(role == 2, d, e)))

    def look(table, i):
        value = jnp.int32(0)
        for k, row in enumerate(table):
            value = jnp.where(i == k, pick(row), value)
        return value

    def half(ref, k):
        return ref.at[pl.ds(k * chunk, chunk)]

    def remote(src, dst, send, recv, device):
        return pltpu.make_async_remote_copy(
            src_ref=src, dst_ref=dst, send_sem=send, recv_sem=recv, device_id=device, device_id_type=MESH
        )

    rounds = (8, 4, depth)
    seats = (2 * y + c, x, z)

    def peer(r, d):
        seat = lax.rem(seats[r] + d, rounds[r])
        if r == 0:
            return (p - c + lax.rem(seat, 2), h * 4 + seat // 2)
        if r == 1:
            return (z * 4 + lax.rem(seat, 2) * 2 + c, (seat // 2) * 4 + y)
        return (seat * 4 + lax.rem(p, 4), g)

    image_load = pltpu.make_async_copy(image_hbm, image_ref, load_sem.at[0])
    text_load = pltpu.make_async_copy(text_hbm, text_ref, load_sem.at[1])
    image_load.start()
    text_load.start()

    barrier = pltpu.get_barrier_semaphore()
    greeted = [along_y(1), along_y(-1)]
    greeted += [place(dz, dx, core) for dz, dx in ((0, 1), (0, -1), (1, 0), (-1, 0)) for core in (0, 1)]
    greeted += [peer(r, d) for r in range(3) for d in range(1, rounds[r])]
    for device in greeted:
        pl.semaphore_signal(barrier, inc=1, device_id=device, device_id_type=MESH)

    image_load.wait()
    images[c, 0] = normalize(image_ref[...])[0].astype(jnp.bfloat16)
    text_load.wait()
    own_text[...] = normalize(text_ref[...])[0].astype(jnp.bfloat16)

    pl.semaphore_wait(barrier, len(greeted))

    def ring(k):
        slot, part, to, into = ((0, 0, 1, 3), (0, 1, -1, 1), (0, 1, 1, 3), (0, 0, -1, 1), (3, 0, 1, 2), (1, 1, -1, 2))[k]
        return remote(
            half(images.at[c, slot], part), half(images.at[c, into], part),
            ring_send.at[k], ring_recv.at[into, part], along_y(to),
        )

    def ring_arrival(slot, part):
        remote(
            half(images.at[c, slot], part), half(images.at[c, slot], part),
            ring_send.at[0], ring_recv.at[slot, part], sibling,
        ).wait_recv()

    def share(slot):
        return remote(images.at[c, slot], images.at[c, slot], share_send.at[slot], share_recv.at[slot], sibling)

    far = low == 1
    first_hops = (
        (place(0, 0, h), 3 + c, c != h),
        (place(0, jnp.where(far & (c == 1), -1, 1), h), jnp.where(far, 5, 1 + c), None),
        (place(jnp.where(far, 1, 0), jnp.where(far, 0, -1), h), jnp.where(far, jnp.where(c == 0, 5, 0), 1 + c), None),
        (place(1, 0, h), 0, jnp.logical_not(far) & (c == 1)),
    )

    def first(k, part):
        device, into, _ = first_hops[k]
        return remote(
            half(own_text, part), half(texts.at[into], part), first_send.at[k, part], text_recv.at[into, part], device
        )

    hands = (
        (pick((5, 2, 5, 1)), place(0, pick((-1, 1, 1, -1)), c), pick((4, 4, 3, 3))),
        (pick((5, 5, 5, 4)), place(pick((1, 0, 1, 1)), pick((0, -1, 0, 0)), c), pick((2, 1, 1, 0))),
        (pick((0, 0, 4, 4)), place(pick((0, 0, 1, 1)), pick((0, 1, 0, 0)), c), pick((2, 2, 0, 0))),
    )

    def hand(k, part):
        slot, device, into = hands[k]
        return remote(
            half(texts.at[slot], part), half(texts.at[into], part), hand_send.at[k, part], text_recv.at[into, part], device
        )

    def text_arrival(slot, part):
        remote(
            half(own_text, part), half(texts.at[slot], part), first_send.at[0, 0], text_recv.at[slot, part], sibling
        ).wait_recv()

    def when(condition, action):
        if condition is None:
            action()
        else:
            pl.when(condition)(action)

    for part in range(2):
        ring(2 * part).start()
        ring(2 * part + 1).start()
        for k in (1, 2, 3, 0):
            when(first_hops[k][2], lambda k=k, part=part: first(k, part).start())
    share(0).start()

    @pl.when(c == h)
    def _():
        texts[3 + c] = own_text[...]

    parts[pl.ds(5, 2)] = jnp.zeros((2, rows, width), jnp.float32)
    acc[...] = jnp.zeros_like(acc)

    for part in range(2):
        text_arrival(hands[0][0], part)
        hand(0, part).start()

        @pl.when(role == 1)
        def _():
            text_arrival(5, part)

        @pl.when(role < 3)
        def _():
            hand(1, part).start()

        @pl.when(role == 1)
        def _():
            text_arrival(0, part)
            hand(2, part).start()

        if part == 0:
            ring_arrival(3, 0)
            ring(4).start()
            ring_arrival(1, 1)
            ring(5).start()

    ring_arrival(3, 1)
    share(3).start()
    ring_arrival(1, 0)
    share(1).start()
    for part in range(2):

        @pl.when(role >= 2)
        def _():
            text_arrival(4, part)

        @pl.when(role == 2)
        def _():
            hand(2, part).start()

        @pl.when(role == 3)
        def _():
            hand(1, part).start()

    ring_arrival(2, 0)
    ring_arrival(2, 1)
    share(2).start()
    for slot in (0, 1, 3, 2):
        remote(
            images.at[c, slot], images.at[1 - c, slot], share_send.at[slot], share_recv.at[slot], sibling
        ).wait_recv()

    scale = jnp.exp(scale_ref[0])
    offset = bias_ref[0]
    strip = 32
    line = lax.broadcasted_iota(jnp.int32, (strip, rows), 0)
    column = lax.broadcasted_iota(jnp.int32, (strip, rows), 1)

    def fold(values):
        return values.reshape(-1, 8, rows).sum(axis=0)

    def tile(s, lane, into, paired, sums):
        losses, scales, biases = sums
        for k in range(rows // strip):
            lines = pl.ds(k * strip, strip)
            logits = scores[lines, pl.ds(lane, rows)]
            score = scale * logits + offset
            if paired is not None:
                match = (line + k * strip == column) & paired
                score = jnp.where(match, -score, score)
            small = jnp.exp(-jnp.abs(score))
            whole = 1.0 + small
            inverse = 1.0 / whole
            loss = jnp.maximum(score, 0.0) + (jnp.log(whole) + (small - (whole - 1.0)) * inverse)
            slope = jnp.where(score >= 0.0, 1.0, small) * inverse
            if paired is not None:
                slope = jnp.where(match, -slope, slope)
            weights[s, lines, into] = (scale * slope).astype(jnp.bfloat16)
            losses += fold(loss)
            scales += fold(slope * logits)
            biases += fold(slope)
        return losses, scales, biases

    def pairs_of(s, block, tiles, first_lane, paired):
        scores[:, pl.ds(0, tiles * rows)] = dot(texts[s], block, NT)
        sums = (acc[0], acc[1], acc[2])
        for t in range(tiles):
            if isinstance(first_lane, int):
                into = pl.ds(first_lane + t * rows, rows)
            else:
                into = pl.ds(pl.multiple_of(first_lane + t * rows, rows), rows)
            sums = tile(s, t * rows, into, paired if t == 0 else None, sums)
        acc[0], acc[1], acc[2] = sums
        if isinstance(first_lane, int):
            used = weights[s, :, pl.ds(first_lane, tiles * rows)]
        else:
            used = weights[s, :, pl.ds(pl.multiple_of(first_lane, tiles * rows), tiles * rows)]
        parts[s] = dot(used, block, NN)

    strip_rows = 16

    def lines_of(part, i):
        return pl.ds(pl.multiple_of(part * chunk + i * strip_rows, strip_rows), strip_rows)

    def strips(action):
        def body(i, carry):
            action(i)
            return carry

        lax.fori_loop(0, chunk // strip_rows, body, 0, unroll=2)

    def pack(value, wire, into):
        code, step = encode(value)
        wire[into + (pl.ds(0, width),)] = code
        wire[into + (pl.ds(width, 128),)] = jnp.broadcast_to(step, (strip_rows, 128))

    def unpack(wire, at):
        return decode(wire[at + (pl.ds(0, width),)], wire[at + (pl.ds(width, 128),)][:, 0:1])

    def part_copy(i, part):
        core = look(PART_CORE, i)
        device = place(look(PART_Z, i), look(PART_X, i), jnp.where(core == 2, c, core))
        s, into = look(ORDER, i), look(PART_SLOT, i)
        return remote(
            half(wires.at[s], part), half(inbox.at[into], part), part_send.at[i, part], part_recv.at[into, part], device
        )

    def part_sent(i):
        kind = look(SENT, i)
        return (kind == 1) | ((kind == 2) & (c == 1)) | ((kind == 3) & (c == 0))

    def text_step(i, carry):
        s = look(ORDER, i)
        sent = part_sent(i)

        @pl.when(sent)
        def _():
            text_arrival(s, 0)
            text_arrival(s, 1)

        middle = (s > 0) & (s < 4)

        @pl.when(middle)
        def _():
            pairs_of(s, images[...].reshape(8 * rows, width), 8, 0, (c == h) & (s == 3))

        @pl.when(jnp.logical_not(middle))
        def _():
            b = jnp.where(s == 4, 1, 0)
            pairs_of(s, images[b].reshape(4 * rows, width), 4, b * 4 * rows, (c == h) & (s == 4))

        @pl.when(sent)
        def _():
            for part in range(2):

                def code(k):
                    lines = lines_of(part, k)
                    pack(parts[s, lines], wires, (s, lines))

                strips(code)
                part_copy(i, part).start()

        return carry

    lax.fori_loop(0, 5, text_step, 0)

    def image_sum(b, slot):
        lanes = pl.ds(pl.multiple_of((4 * b + slot) * rows, rows), rows)
        lhs = weights[pl.ds(b, 4), :, lanes].reshape(4 * rows, rows)
        rhs = texts[pl.ds(b, 4)].reshape(4 * rows, width)
        return dot(lhs, rhs, TN)

    def core_copy(slot):
        return remote(image_other.at[slot], core_in.at[slot], core_send.at[slot], core_recv.at[slot], sibling)

    def other_step(i, carry):
        slot = lax.rem(i + 2, 4)
        image_other[slot] = image_sum(1 - c, slot)
        core_copy(slot).start()
        return carry

    lax.fori_loop(0, 4, other_step, 0)

    def own_step(i, carry):
        slot = lax.rem(i + 2, 4)
        image_part[slot] = image_sum(c, slot)
        return carry

    lax.fori_loop(0, 4, own_step, 0)

    def back(k):
        slot, part, to, dst, sem = (
            (2, 0, 1, half(relay, 0), relay_recv.at[0]),
            (2, 1, -1, half(relay, 1), relay_recv.at[1]),
            (1, 1, 1, half(image_in.at[0], 1), image_recv.at[0, 1]),
            (3, 0, -1, half(image_in.at[1], 0), image_recv.at[1, 0]),
            (1, 0, 1, half(image_in.at[0], 0), image_recv.at[0, 0]),
            (3, 1, -1, half(image_in.at[1], 1), image_recv.at[1, 1]),
        )[k]
        return remote(half(back_wires.at[slot], part), dst, back_send.at[k], sem, along_y(to))

    def back_start(k, slot, part, add=None):
        def code(i):
            lines = lines_of(part, i)
            value = image_part[slot, lines]
            if add is not None:
                value += unpack(add, (lines,))
            pack(value, back_wires, (slot, lines))

        strips(code)
        back(k).start()

    for slot, ready in ((2, ((0, 0), (1, 1))), (3, ((3, 0),)), (1, ((2, 1),)), (0, ())):
        core_copy(slot).wait_recv()
        image_part[slot] += core_in[slot]
        for k, part in ready:
            back_start(k, slot, part)

    lates = (
        (pick((5, 0, 4, 4)), 0, place(pick((0, -1, 0, 0)), pick((1, 0, -1, 1)), jnp.where(role < 2, 1, c)), pick((4, 5, 2, 0))),
        (pick((5, 5, 5, 1)), pick((1, 1, 2, 1)), place(pick((0, -1, 0, 0)), pick((0, 0, -1, 1)), 0), pick((5, 5, 4, 5))),
        (2, 2, place(0, -1, 1), 4),
    )
    late_on = (None, role > 0, role == 1)

    def late(k, part):
        _, _, device, into = lates[k]
        return remote(
            half(late_wires.at[k], part), half(inbox.at[into], part), late_send.at[k, part], part_recv.at[into, part], device
        )

    def part_arrival(slot, part):
        remote(
            half(inbox.at[slot], part), half(inbox.at[slot], part), late_send.at[0, 0], part_recv.at[slot, part], sibling
        ).wait_recv()

    def absorb(into, slot, part):
        def add(i):
            lines = lines_of(part, i)
            parts[into, lines] += unpack(inbox, (slot, lines))

        strips(add)

    def late_start(k, part):
        into, slot, _, _ = lates[k]

        def add(i):
            lines = lines_of(part, i)
            pack(parts[into, lines] + unpack(inbox, (slot, lines)), late_wires, (k, lines))

        strips(add)
        late(k, part).start()

    def late_0(part):
        @pl.when(role == 0)
        def _():
            part_arrival(1, part)
            absorb(5, 1, part)

        part_arrival(0, part)
        late_start(0, part)

    def late_1(part):
        part_arrival(1, part)

        @pl.when(role == 2)
        def _():
            absorb(5, 1, part)
            part_arrival(2, part)

        late_start(1, part)

    def late_2(part):
        part_arrival(2, part)
        late_start(2, part)

    def total_copy(r, d):
        seat = seats[r]
        return remote(
            totals.at[r, seat], totals.at[r, seat], total_send.at[r, d - 1], total_recv.at[r, seat], peer(r, d)
        )

    def total_sum(r):
        for d in range(1, rounds[r]):
            seat = lax.rem(seats[r] + d, rounds[r])
            remote(
                totals.at[r, seat], totals.at[r, seat], total_send.at[r, d - 1], total_recv.at[r, seat], sibling
            ).wait_recv()
        value = totals[r, 0]
        for seat in range(1, rounds[r]):
            value += totals[r, seat]
        return value

    def total_start(r, value):
        totals[r, seats[r]] = value
        for d in range(1, rounds[r]):
            total_copy(r, d).start()

    def relayed(k):
        slot, part = ((1, 0), (3, 1))[k]
        remote(half(relay, k), half(relay, k), back_send.at[0], relay_recv.at[k], sibling).wait_recv()
        back_start(4 + k, slot, part, relay)

    total_start(0, jnp.concatenate([jnp.sum(acc[k], axis=0, keepdims=True)[None] for k in range(3)], axis=0))
    pl.when(role == 1)(lambda: late_1(0))
    pl.when(role > 1)(lambda: late_0(0))
    pl.when(role == 1)(lambda: late_1(1))
    pl.when(role > 1)(lambda: late_0(1))
    total_start(1, total_sum(0))
    pl.when(role == 1)(lambda: late_0(0))
    pl.when(role > 1)(lambda: late_1(0))
    relayed(0)
    relayed(1)
    total_start(2, total_sum(1))
    pl.when(role == 1)(lambda: late_0(1))
    pl.when(role > 1)(lambda: late_1(1))
    pl.when(role == 0)(lambda: late_0(0))
    pl.when(role == 1)(lambda: late_2(0))
    pl.when(role == 0)(lambda: late_0(1))
    pl.when(role == 1)(lambda: late_2(1))
    total = jnp.sum(total_sum(2), axis=-1, keepdims=True)
    pairs = float(n_blk * n_grp * rows * STEPS * n_grp * rows)
    sums_ref[0:1, :] = jnp.broadcast_to(total[0] / pairs, (1, 128))
    sums_ref[1:2, :] = jnp.broadcast_to(total[1] * scale / pairs, (1, 128))
    sums_ref[2:3, :] = jnp.broadcast_to(total[2] / pairs, (1, 128))

    for part in range(2):
        for slot in range(2):
            remote(
                half(image_in.at[slot], part), half(image_in.at[slot], part),
                back_send.at[0], image_recv.at[slot, part], sibling,
            ).wait_recv()

        def last(i):
            lines = lines_of(part, i)
            total = image_part[0, lines] + unpack(image_in, (0, lines)) + unpack(image_in, (1, lines))
            grad_image_ref[lines] = finish(image_ref[lines], total)

        strips(last)

    extra = jnp.logical_not(far) & (c == 1)
    own = jnp.where(c == h, 3 + c, 6)
    for part in range(2):

        @pl.when(c != h)
        def _():
            part_arrival(3, part)
            absorb(6, 3, part)

        part_arrival(4, part)

        @pl.when(extra)
        def _():
            part_arrival(6, part)
            absorb(own, 6, part)

        part_arrival(5, part)

        def last(i):
            lines = lines_of(part, i)
            total = parts[own, lines] + unpack(inbox, (4, lines)) + unpack(inbox, (5, lines))
            grad_text_ref[lines] = finish(text_ref[lines], total)

        strips(last)

    for k in range(6):
        ring(k).wait_send()
        back(k).wait_send()
    for slot in range(4):
        share(slot).wait_send()
        core_copy(slot).wait_send()
    for part in range(2):
        for k in range(4):
            when(first_hops[k][2], lambda k=k, part=part: first(k, part).wait_send())
        hand(0, part).wait_send()
        hand(1, part).wait_send()
        pl.when((role == 1) | (role == 2))(lambda part=part: hand(2, part).wait_send())
        for k in range(3):
            when(late_on[k], lambda k=k, part=part: late(k, part).wait_send())

    def drain(i, carry):
        @pl.when(part_sent(i))
        def _():
            part_copy(i, 0).wait_send()
            part_copy(i, 1).wait_send()

        return carry

    lax.fori_loop(0, 5, drain, 0)
    for r in range(3):
        for d in range(1, rounds[r]):
            total_copy(r, d).wait_send()


def local(n_blk, n_grp, image_embed, text_embed, log_scale, bias):
    rows, width = image_embed.shape
    low, wide = jnp.bfloat16, jnp.float32
    dma = pltpu.SemaphoreType.DMA
    vmem = pl.BlockSpec(memory_space=pltpu.VMEM)
    smem = pl.BlockSpec(memory_space=pltpu.SMEM)
    hbm = pl.BlockSpec(memory_space=pltpu.HBM)
    out = jax.ShapeDtypeStruct((rows, width), wide)
    pairs = n_grp * rows * STEPS * rows
    grad_image, grad_text, sums = pl.pallas_call(
        functools.partial(kernel, n_blk, n_grp),
        out_shape=(out, out, jax.ShapeDtypeStruct((8, 128), wide)),
        in_specs=[smem, smem, hbm, hbm],
        out_specs=(vmem, vmem, vmem),
        scratch_shapes=[
            pltpu.VMEM((rows, width), low),
            pltpu.VMEM((rows, width), low),
            dma((2,)),
            pltpu.VMEM((2, 4, rows, width), low),
            pltpu.VMEM((6, rows, width), low),
            pltpu.VMEM((rows, width), low),
            pltpu.VMEM((rows, 8 * rows), wide),
            pltpu.VMEM((5, rows, 8 * rows), low),
            pltpu.VMEM((7, rows, width), wide),
            pltpu.VMEM((5, rows, width + 128), low),
            pltpu.VMEM((7, rows, width + 128), low),
            pltpu.VMEM((3, rows, width + 128), low),
            pltpu.VMEM((4, rows, width), wide),
            pltpu.VMEM((4, rows, width), wide),
            pltpu.VMEM((4, rows, width), wide),
            pltpu.VMEM((4, rows, width + 128), low),
            pltpu.VMEM((rows, width + 128), low),
            pltpu.VMEM((2, rows, width + 128), low),
            pltpu.VMEM((3, 8, 128), wide),
            pltpu.VMEM((3, 8, 3, 1, 128), wide),
            dma((6,)), dma((4, 2)), dma((4,)), dma((4,)), dma((4, 2)), dma((3, 2)), dma((6, 2)),
            dma((5, 2)), dma((3, 2)), dma((7, 2)), dma((4,)), dma((4,)), dma((6,)), dma((2,)), dma((2, 2)),
            dma((3, 8)), dma((3, 8)),
        ],
        compiler_params=pltpu.CompilerParams(
            collective_id=0, has_side_effects=True, vmem_limit_bytes=48 << 20
        ),
        cost_estimate=pl.CostEstimate(
            flops=6 * pairs * width, bytes_accessed=12 * rows * width, transcendentals=3 * pairs
        ),
        name="pair_loss",
    )(log_scale, bias, image_embed, text_embed)
    return grad_image, grad_text, sums[0, 0], sums[1, 0], sums[2, 0]


def solution(mesh):
    split = P(("blk", "grp"), None)
    return jax.shard_map(
        functools.partial(local, mesh.shape["blk"], mesh.shape["grp"]),
        mesh=mesh,
        in_specs=(split, split, P(), P()),
        out_specs=(split, split, P(), P(), P()),
        check_vma=False,
    )
```

```python
import functools

import jax
import jax.numpy as jnp
from jax import lax
from jax.experimental import pallas as pl
from jax.experimental.pallas import tpu as pltpu
from jax.sharding import PartitionSpec as P

MESH = pl.DeviceIdType.MESH
STEPS = 4
ROUND = 12582912.0
NT = (((1,), (1,)), ((), ()))
TN = (((0,), (0,)), ((), ()))
NN = (((1,), (0,)), ((), ()))

ORDER = ((2, 1, 1, 3), (1, 0, 3, 2), (0, 2, 2, 0), (3, 3, 0, 4), (4, 4, 4, 1))
PART_Z = ((-1, 0, -1, 0), (0, 0, 0, 0), (-1, 0, 0, -1), (0, 0, -1, 0), (0, 0, 0, 0))
PART_X = ((0, -1, 0, -1), (1, 0, 1, 1), (0, 0, -1, 0), (0, 0, 0, 0), (0, 0, 0, 0))
PART_CORE = ((2, 0, 2, 2), (2, 2, 2, 1), (1, 2, 2, 2), (0, 0, 2, 2), (1, 1, 2, 2))
PART_SLOT = ((1, 4, 1, 2), (1, 0, 1, 5), (6, 0, 0, 0), (3, 3, 0, 0), (3, 3, 0, 0))
SENT = ((1, 1, 1, 1), (1, 0, 1, 1), (1, 0, 1, 1), (2, 2, 1, 0), (3, 3, 0, 0))


def normalize(embed):
    wide = embed.astype(jnp.float32)
    inverse = lax.rsqrt(jnp.sum(wide * wide, axis=1, keepdims=True) + 1e-06)
    return wide * inverse, inverse


def finish(embed, back):
    unit, inverse = normalize(embed)
    return inverse * (back - unit * jnp.sum(unit * back, axis=1, keepdims=True))


def encode(value):
    top = jnp.max(jnp.abs(value), axis=1, keepdims=True)
    step = (jnp.maximum(top, 1e-30) * (1.008 / 16383.0)).astype(jnp.bfloat16).astype(jnp.float32)
    whole = (value * (1.0 / step) + ROUND) - ROUND
    upper = jnp.floor(whole * (1.0 / 128.0))
    lower = whole - 128.0 * upper
    signed = jnp.where(upper >= 0.0, upper + 128.0, upper - 127.0)
    return (signed * jnp.exp2(lower - 71.0)).astype(jnp.bfloat16), step.astype(jnp.bfloat16)


def decode(code, step):
    wide = code.astype(jnp.float32)
    size = jnp.abs(wide)
    power = jnp.floor(jnp.log2(size) + 0.001)
    mantissa = size * jnp.exp2(7.0 - power)
    upper = jnp.where(wide >= 0.0, mantissa - 128.0, 127.0 - mantissa)
    return (upper * 128.0 + (power + 64.0)) * step.astype(jnp.float32)


def dot(a, b, dims):
    return lax.dot_general(a, b, dims, preferred_element_type=jnp.float32)


def kernel(
    n_blk, n_grp,
    scale_ref, bias_ref, image_hbm, text_hbm,
    grad_image_ref, grad_text_ref, sums_ref,
    image_ref, text_ref, load_sem, images, texts, own_text, scores, weights, parts, wires, inbox, late_wires,
    image_part, image_other, core_in, back_wires, relay, image_in, acc, totals,
    ring_send, ring_recv, share_send, share_recv, first_send, hand_send, text_recv,
    part_send, late_send, part_recv, core_send, core_recv, back_send, relay_recv, image_recv,
    total_send, total_recv,
):
    rows, width = image_ref.shape
    chunk = rows // 2
    p = lax.axis_index("blk")
    g = lax.axis_index("grp")
    c = lax.rem(p, 2)
    z = p // 4
    low = lax.rem(p // 2, 2)
    h = g // 4
    y = lax.rem(g, 4)
    x = 2 * h + low
    role = lax.rem(x + 4 - 2 * c, 4)
    depth = n_blk // 4

    def place(dz, dx, core):
        at_x = lax.rem(x + dx + 4, 4)
        at_z = lax.rem(z + dz + depth, depth)
        return (at_z * 4 + lax.rem(at_x, 2) * 2 + core, (at_x // 2) * 4 + y)

    def along_y(d):
        return (p, h * 4 + lax.rem(y + d + 4, 4))

    sibling = (p + 1 - 2 * c, g)

    def pick(row):
        a, b, d, e = row
        return jnp.where(role == 0, a, jnp.where(role == 1, b, jnp.where(role == 2, d, e)))

    def look(table, i):
        value = jnp.int32(0)
        for k, row in enumerate(table):
            value = jnp.where(i == k, pick(row), value)
        return value

    def half(ref, k):
        return ref.at[pl.ds(k * chunk, chunk)]

    def remote(src, dst, send, recv, device):
        return pltpu.make_async_remote_copy(
            src_ref=src, dst_ref=dst, send_sem=send, recv_sem=recv, device_id=device, device_id_type=MESH
        )

    rounds = (8, 4, depth)
    seats = (2 * y + c, x, z)

    def peer(r, d):
        seat = lax.rem(seats[r] + d, rounds[r])
        if r == 0:
            return (p - c + lax.rem(seat, 2), h * 4 + seat // 2)
        if r == 1:
            return (z * 4 + lax.rem(seat, 2) * 2 + c, (seat // 2) * 4 + y)
        return (seat * 4 + lax.rem(p, 4), g)

    image_load = pltpu.make_async_copy(image_hbm, image_ref, load_sem.at[0])
    text_load = pltpu.make_async_copy(text_hbm, text_ref, load_sem.at[1])
    image_load.start()
    text_load.start()

    barrier = pltpu.get_barrier_semaphore()
    greeted = [along_y(1), along_y(-1)]
    greeted += [place(dz, dx, core) for dz, dx in ((0, 1), (0, -1), (1, 0), (-1, 0)) for core in (0, 1)]
    greeted += [peer(r, d) for r in range(3) for d in range(1, rounds[r])]
    for device in greeted:
        pl.semaphore_signal(barrier, inc=1, device_id=device, device_id_type=MESH)

    image_load.wait()
    images[c, 0] = normalize(image_ref[...])[0].astype(jnp.bfloat16)
    text_load.wait()
    own_text[...] = normalize(text_ref[...])[0].astype(jnp.bfloat16)

    pl.semaphore_wait(barrier, len(greeted))

    def ring(k):
        slot, part, to, into = ((0, 0, 1, 3), (0, 1, -1, 1), (0, 1, 1, 3), (0, 0, -1, 1), (3, 0, 1, 2), (1, 1, -1, 2))[k]
        return remote(
            half(images.at[c, slot], part), half(images.at[c, into], part),
            ring_send.at[k], ring_recv.at[into, part], along_y(to),
        )

    def ring_arrival(slot, part):
        remote(
            half(images.at[c, slot], part), half(images.at[c, slot], part),
            ring_send.at[0], ring_recv.at[slot, part], sibling,
        ).wait_recv()

    def share(slot):
        return remote(images.at[c, slot], images.at[c, slot], share_send.at[slot], share_recv.at[slot], sibling)

    far = low == 1
    first_hops = (
        (place(0, 0, h), 3 + c, c != h),
        (place(0, jnp.where(far & (c == 1), -1, 1), h), jnp.where(far, 5, 1 + c), None),
        (place(jnp.where(far, 1, 0), jnp.where(far, 0, -1), h), jnp.where(far, jnp.where(c == 0, 5, 0), 1 + c), None),
        (place(1, 0, h), 0, jnp.logical_not(far) & (c == 1)),
    )

    def first(k, part):
        device, into, _ = first_hops[k]
        return remote(
            half(own_text, part), half(texts.at[into], part), first_send.at[k, part], text_recv.at[into, part], device
        )

    hands = (
        (pick((5, 2, 5, 1)), place(0, pick((-1, 1, 1, -1)), c), pick((4, 4, 3, 3))),
        (pick((5, 5, 5, 4)), place(pick((1, 0, 1, 1)), pick((0, -1, 0, 0)), c), pick((2, 1, 1, 0))),
        (pick((0, 0, 4, 4)), place(pick((0, 0, 1, 1)), pick((0, 1, 0, 0)), c), pick((2, 2, 0, 0))),
    )

    def hand(k, part):
        slot, device, into = hands[k]
        return remote(
            half(texts.at[slot], part), half(texts.at[into], part), hand_send.at[k, part], text_recv.at[into, part], device
        )

    def text_arrival(slot, part):
        remote(
            half(own_text, part), half(texts.at[slot], part), first_send.at[0, 0], text_recv.at[slot, part], sibling
        ).wait_recv()

    def when(condition, action):
        if condition is None:
            action()
        else:
            pl.when(condition)(action)

    for part in range(2):
        ring(2 * part).start()
        ring(2 * part + 1).start()
        for k in (1, 2, 3, 0):
            when(first_hops[k][2], lambda k=k, part=part: first(k, part).start())
    share(0).start()

    @pl.when(c == h)
    def _():
        texts[3 + c] = own_text[...]

    parts[pl.ds(5, 2)] = jnp.zeros((2, rows, width), jnp.float32)
    acc[...] = jnp.zeros_like(acc)

    for part in range(2):
        text_arrival(hands[0][0], part)
        hand(0, part).start()

        @pl.when(role == 1)
        def _():
            text_arrival(5, part)

        @pl.when(role < 3)
        def _():
            hand(1, part).start()

        @pl.when(role == 1)
        def _():
            text_arrival(0, part)
            hand(2, part).start()

        if part == 0:
            ring_arrival(3, 0)
            ring(4).start()
            ring_arrival(1, 1)
            ring(5).start()

    ring_arrival(3, 1)
    share(3).start()
    ring_arrival(1, 0)
    share(1).start()
    for part in range(2):

        @pl.when(role >= 2)
        def _():
            text_arrival(4, part)

        @pl.when(role == 2)
        def _():
            hand(2, part).start()

        @pl.when(role == 3)
        def _():
            hand(1, part).start()

    ring_arrival(2, 0)
    ring_arrival(2, 1)
    share(2).start()
    for slot in (0, 1, 3, 2):
        remote(
            images.at[c, slot], images.at[1 - c, slot], share_send.at[slot], share_recv.at[slot], sibling
        ).wait_recv()

    scale = jnp.exp(scale_ref[0])
    offset = bias_ref[0]
    strip = 32
    line = lax.broadcasted_iota(jnp.int32, (strip, rows), 0)
    column = lax.broadcasted_iota(jnp.int32, (strip, rows), 1)

    def fold(values):
        return values.reshape(-1, 8, rows).sum(axis=0)

    def tile(s, lane, into, paired, sums):
        losses, scales, biases = sums
        for k in range(rows // strip):
            lines = pl.ds(k * strip, strip)
            logits = scores[lines, pl.ds(lane, rows)]
            score = scale * logits + offset
            if paired is not None:
                match = (line + k * strip == column) & paired
                score = jnp.where(match, -score, score)
            small = jnp.exp(-jnp.abs(score))
            whole = 1.0 + small
            inverse = 1.0 / whole
            loss = jnp.maximum(score, 0.0) + (jnp.log(whole) + (small - (whole - 1.0)) * inverse)
            slope = jnp.where(score >= 0.0, 1.0, small) * inverse
            if paired is not None:
                slope = jnp.where(match, -slope, slope)
            weights[s, lines, into] = (scale * slope).astype(jnp.bfloat16)
            losses += fold(loss)
            scales += fold(slope * logits)
            biases += fold(slope)
        return losses, scales, biases

    def pairs_of(s, block, tiles, first_lane, paired):
        scores[:, pl.ds(0, tiles * rows)] = dot(texts[s], block, NT)
        sums = (acc[0], acc[1], acc[2])
        for t in range(tiles):
            if isinstance(first_lane, int):
                into = pl.ds(first_lane + t * rows, rows)
            else:
                into = pl.ds(pl.multiple_of(first_lane + t * rows, rows), rows)
            sums = tile(s, t * rows, into, paired if t == 0 else None, sums)
        acc[0], acc[1], acc[2] = sums
        if isinstance(first_lane, int):
            used = weights[s, :, pl.ds(first_lane, tiles * rows)]
        else:
            used = weights[s, :, pl.ds(pl.multiple_of(first_lane, tiles * rows), tiles * rows)]
        parts[s] = dot(used, block, NN)

    strip_rows = 32

    def lines_of(part, i):
        return pl.ds(pl.multiple_of(part * chunk + i * strip_rows, strip_rows), strip_rows)

    def strips(action):
        def body(i, carry):
            action(i)
            return carry

        lax.fori_loop(0, chunk // strip_rows, body, 0, unroll=2)

    def pack(value, wire, into):
        code, step = encode(value)
        wire[into + (pl.ds(0, width),)] = code
        wire[into + (pl.ds(width, 128),)] = jnp.broadcast_to(step, (strip_rows, 128))

    def unpack(wire, at):
        return decode(wire[at + (pl.ds(0, width),)], wire[at + (pl.ds(width, 128),)][:, 0:1])

    def part_copy(i, part):
        core = look(PART_CORE, i)
        device = place(look(PART_Z, i), look(PART_X, i), jnp.where(core == 2, c, core))
        s, into = look(ORDER, i), look(PART_SLOT, i)
        return remote(
            half(wires.at[s], part), half(inbox.at[into], part), part_send.at[i, part], part_recv.at[into, part], device
        )

    def part_sent(i):
        kind = look(SENT, i)
        return (kind == 1) | ((kind == 2) & (c == 1)) | ((kind == 3) & (c == 0))

    def text_step(i, carry):
        s = look(ORDER, i)
        sent = part_sent(i)

        @pl.when(sent)
        def _():
            text_arrival(s, 0)
            text_arrival(s, 1)

        middle = (s > 0) & (s < 4)

        @pl.when(middle)
        def _():
            pairs_of(s, images[...].reshape(8 * rows, width), 8, 0, (c == h) & (s == 3))

        @pl.when(jnp.logical_not(middle))
        def _():
            b = jnp.where(s == 4, 1, 0)
            pairs_of(s, images[b].reshape(4 * rows, width), 4, b * 4 * rows, (c == h) & (s == 4))

        @pl.when(sent)
        def _():
            for part in range(2):

                def code(k):
                    lines = lines_of(part, k)
                    pack(parts[s, lines], wires, (s, lines))

                strips(code)
                part_copy(i, part).start()

        return carry

    lax.fori_loop(0, 5, text_step, 0)

    def total_copy(r, d):
        seat = seats[r]
        return remote(
            totals.at[r, seat], totals.at[r, seat], total_send.at[r, d - 1], total_recv.at[r, seat], peer(r, d)
        )

    def total_sum(r):
        for d in range(1, rounds[r]):
            seat = lax.rem(seats[r] + d, rounds[r])
            remote(
                totals.at[r, seat], totals.at[r, seat], total_send.at[r, d - 1], total_recv.at[r, seat], sibling
            ).wait_recv()
        value = totals[r, 0]
        for seat in range(1, rounds[r]):
            value += totals[r, seat]
        return value

    def total_start(r, value):
        totals[r, seats[r]] = value
        for d in range(1, rounds[r]):
            total_copy(r, d).start()

    total_start(0, jnp.concatenate([jnp.sum(acc[k], axis=0, keepdims=True)[None] for k in range(3)], axis=0))

    def image_sum(b, slot):
        lanes = pl.ds(pl.multiple_of((4 * b + slot) * rows, rows), rows)
        lhs = weights[pl.ds(b, 4), :, lanes].reshape(4 * rows, rows)
        rhs = texts[pl.ds(b, 4)].reshape(4 * rows, width)
        return dot(lhs, rhs, TN)

    def core_copy(slot):
        return remote(image_other.at[slot], core_in.at[slot], core_send.at[slot], core_recv.at[slot], sibling)

    def other_step(i, carry):
        slot = jnp.where(i < 2, 2 + i, 3 - i)
        image_other[slot] = image_sum(1 - c, slot)
        core_copy(slot).start()
        return carry

    lax.fori_loop(0, 4, other_step, 0)

    def own_step(i, carry):
        slot = jnp.where(i < 2, 2 + i, 3 - i)
        image_part[slot] = image_sum(c, slot)
        return carry

    lax.fori_loop(0, 4, own_step, 0)
    total_start(1, total_sum(0))

    def back(k):
        slot, part, to, dst, sem = (
            (2, 0, 1, half(relay, 0), relay_recv.at[0]),
            (2, 1, -1, half(relay, 1), relay_recv.at[1]),
            (1, 1, 1, half(image_in.at[0], 1), image_recv.at[0, 1]),
            (3, 0, -1, half(image_in.at[1], 0), image_recv.at[1, 0]),
            (1, 0, 1, half(image_in.at[0], 0), image_recv.at[0, 0]),
            (3, 1, -1, half(image_in.at[1], 1), image_recv.at[1, 1]),
        )[k]
        return remote(half(back_wires.at[slot], part), dst, back_send.at[k], sem, along_y(to))

    def back_start(k, slot, part, add=None):
        def code(i):
            lines = lines_of(part, i)
            value = image_part[slot, lines]
            if add is not None:
                value += unpack(add, (lines,))
            pack(value, back_wires, (slot, lines))

        strips(code)
        back(k).start()

    for slot, ready in ((2, ((0, 0), (1, 1))), (3, ((3, 0),)), (1, ((2, 1),)), (0, ())):
        core_copy(slot).wait_recv()
        image_part[slot] += core_in[slot]
        for k, part in ready:
            back_start(k, slot, part)

    lates = (
        (pick((5, 0, 4, 4)), 0, place(pick((0, -1, 0, 0)), pick((1, 0, -1, 1)), jnp.where(role < 2, 1, c)), pick((4, 5, 2, 0))),
        (pick((5, 5, 5, 1)), pick((1, 1, 2, 1)), place(pick((0, -1, 0, 0)), pick((0, 0, -1, 1)), 0), pick((5, 5, 4, 5))),
        (2, 2, place(0, -1, 1), 4),
    )
    late_on = (None, role > 0, role == 1)

    def late(k, part):
        _, _, device, into = lates[k]
        return remote(
            half(late_wires.at[k], part), half(inbox.at[into], part), late_send.at[k, part], part_recv.at[into, part], device
        )

    def part_arrival(slot, part):
        remote(
            half(inbox.at[slot], part), half(inbox.at[slot], part), late_send.at[0, 0], part_recv.at[slot, part], sibling
        ).wait_recv()

    def absorb(into, slot, part):
        def add(i):
            lines = lines_of(part, i)
            parts[into, lines] += unpack(inbox, (slot, lines))

        strips(add)

    def late_start(k, part):
        into, slot, _, _ = lates[k]

        def add(i):
            lines = lines_of(part, i)
            pack(parts[into, lines] + unpack(inbox, (slot, lines)), late_wires, (k, lines))

        strips(add)
        late(k, part).start()

    def late_0(part):
        @pl.when(role == 0)
        def _():
            part_arrival(1, part)
            absorb(5, 1, part)

        part_arrival(0, part)
        late_start(0, part)

    def late_1(part):
        part_arrival(1, part)

        @pl.when(role == 2)
        def _():
            absorb(5, 1, part)
            part_arrival(2, part)

        late_start(1, part)

    def late_2(part):
        part_arrival(2, part)
        late_start(2, part)

    def relayed(k):
        slot, part = ((1, 0), (3, 1))[k]
        remote(half(relay, k), half(relay, k), back_send.at[0], relay_recv.at[k], sibling).wait_recv()
        back_start(4 + k, slot, part, relay)

    pl.when(role == 1)(lambda: late_1(0))
    pl.when(role > 1)(lambda: late_0(0))
    pl.when(role == 1)(lambda: late_1(1))
    pl.when(role > 1)(lambda: late_0(1))
    total_start(2, total_sum(1))
    pl.when(role == 1)(lambda: late_0(0))
    pl.when(role > 1)(lambda: late_1(0))
    relayed(0)
    relayed(1)
    pl.when(role == 1)(lambda: late_0(1))
    pl.when(role > 1)(lambda: late_1(1))
    pl.when(role == 0)(lambda: late_0(0))
    pl.when(role == 1)(lambda: late_2(0))
    pl.when(role == 0)(lambda: late_0(1))
    pl.when(role == 1)(lambda: late_2(1))
    total = jnp.sum(total_sum(2), axis=-1, keepdims=True)
    pairs = float(n_blk * n_grp * rows * STEPS * n_grp * rows)
    sums_ref[0:1, :] = jnp.broadcast_to(total[0] / pairs, (1, 128))
    sums_ref[1:2, :] = jnp.broadcast_to(total[1] * scale / pairs, (1, 128))
    sums_ref[2:3, :] = jnp.broadcast_to(total[2] / pairs, (1, 128))

    for part in range(2):
        for slot in range(2):
            remote(
                half(image_in.at[slot], part), half(image_in.at[slot], part),
                back_send.at[0], image_recv.at[slot, part], sibling,
            ).wait_recv()

        def last(i):
            lines = lines_of(part, i)
            total = image_part[0, lines] + unpack(image_in, (0, lines)) + unpack(image_in, (1, lines))
            grad_image_ref[lines] = finish(image_ref[lines], total)

        strips(last)

    extra = jnp.logical_not(far) & (c == 1)
    own = jnp.where(c == h, 3 + c, 6)
    for part in range(2):

        @pl.when(c != h)
        def _():
            part_arrival(3, part)
            absorb(6, 3, part)

        part_arrival(4, part)

        @pl.when(extra)
        def _():
            part_arrival(6, part)
            absorb(own, 6, part)

        part_arrival(5, part)

        def last(i):
            lines = lines_of(part, i)
            total = parts[own, lines] + unpack(inbox, (4, lines)) + unpack(inbox, (5, lines))
            grad_text_ref[lines] = finish(text_ref[lines], total)

        strips(last)

    for k in range(6):
        ring(k).wait_send()
        back(k).wait_send()
    for slot in range(4):
        share(slot).wait_send()
        core_copy(slot).wait_send()
    for part in range(2):
        for k in range(4):
            when(first_hops[k][2], lambda k=k, part=part: first(k, part).wait_send())
        hand(0, part).wait_send()
        hand(1, part).wait_send()
        pl.when((role == 1) | (role == 2))(lambda part=part: hand(2, part).wait_send())
        for k in range(3):
            when(late_on[k], lambda k=k, part=part: late(k, part).wait_send())

    def drain(i, carry):
        @pl.when(part_sent(i))
        def _():
            part_copy(i, 0).wait_send()
            part_copy(i, 1).wait_send()

        return carry

    lax.fori_loop(0, 5, drain, 0)
    for r in range(3):
        for d in range(1, rounds[r]):
            total_copy(r, d).wait_send()


def local(n_blk, n_grp, image_embed, text_embed, log_scale, bias):
    rows, width = image_embed.shape
    low, wide = jnp.bfloat16, jnp.float32
    dma = pltpu.SemaphoreType.DMA
    vmem = pl.BlockSpec(memory_space=pltpu.VMEM)
    smem = pl.BlockSpec(memory_space=pltpu.SMEM)
    hbm = pl.BlockSpec(memory_space=pltpu.HBM)
    out = jax.ShapeDtypeStruct((rows, width), wide)
    pairs = n_grp * rows * STEPS * rows
    grad_image, grad_text, sums = pl.pallas_call(
        functools.partial(kernel, n_blk, n_grp),
        out_shape=(out, out, jax.ShapeDtypeStruct((8, 128), wide)),
        in_specs=[smem, smem, hbm, hbm],
        out_specs=(vmem, vmem, vmem),
        scratch_shapes=[
            pltpu.VMEM((rows, width), low),
            pltpu.VMEM((rows, width), low),
            dma((2,)),
            pltpu.VMEM((2, 4, rows, width), low),
            pltpu.VMEM((6, rows, width), low),
            pltpu.VMEM((rows, width), low),
            pltpu.VMEM((rows, 8 * rows), wide),
            pltpu.VMEM((5, rows, 8 * rows), low),
            pltpu.VMEM((7, rows, width), wide),
            pltpu.VMEM((5, rows, width + 128), low),
            pltpu.VMEM((7, rows, width + 128), low),
            pltpu.VMEM((3, rows, width + 128), low),
            pltpu.VMEM((4, rows, width), wide),
            pltpu.VMEM((4, rows, width), wide),
            pltpu.VMEM((4, rows, width), wide),
            pltpu.VMEM((4, rows, width + 128), low),
            pltpu.VMEM((rows, width + 128), low),
            pltpu.VMEM((2, rows, width + 128), low),
            pltpu.VMEM((3, 8, 128), wide),
            pltpu.VMEM((3, 8, 3, 1, 128), wide),
            dma((6,)), dma((4, 2)), dma((4,)), dma((4,)), dma((4, 2)), dma((3, 2)), dma((6, 2)),
            dma((5, 2)), dma((3, 2)), dma((7, 2)), dma((4,)), dma((4,)), dma((6,)), dma((2,)), dma((2, 2)),
            dma((3, 8)), dma((3, 8)),
        ],
        compiler_params=pltpu.CompilerParams(
            collective_id=0, has_side_effects=True, vmem_limit_bytes=48 << 20
        ),
        cost_estimate=pl.CostEstimate(
            flops=6 * pairs * width, bytes_accessed=12 * rows * width, transcendentals=3 * pairs
        ),
        name="pair_loss",
    )(
        log_scale, bias,
        pltpu.with_memory_space_constraint(image_embed, pltpu.HBM),
        pltpu.with_memory_space_constraint(text_embed, pltpu.HBM),
    )
    return grad_image, grad_text, sums[0, 0], sums[1, 0], sums[2, 0]


def solution(mesh):
    split = P(("blk", "grp"), None)
    return jax.shard_map(
        functools.partial(local, mesh.shape["blk"], mesh.shape["grp"]),
        mesh=mesh,
        in_specs=(split, split, P(), P()),
        out_specs=(split, split, P(), P(), P()),
        check_vma=False,
    )
```

```python
import functools

import jax
import jax.numpy as jnp
from jax import lax
from jax.experimental import pallas as pl
from jax.experimental.pallas import tpu as pltpu
from jax.sharding import PartitionSpec as P

MESH = pl.DeviceIdType.MESH
STEPS = 4
ROUND = 12582912.0
NT = (((1,), (1,)), ((), ()))
TN = (((0,), (0,)), ((), ()))
NN = (((1,), (0,)), ((), ()))

ORDER = ((2, 1, 1, 3), (1, 0, 3, 2), (0, 2, 2, 0), (3, 3, 0, 4), (4, 4, 4, 1))
PART_Z = ((-1, 0, -1, 0), (0, 0, 0, 0), (-1, 0, 0, -1), (0, 0, -1, 0), (0, 0, 0, 0))
PART_X = ((0, -1, 0, -1), (1, 0, 1, 1), (0, 0, -1, 0), (0, 0, 0, 0), (0, 0, 0, 0))
PART_CORE = ((2, 0, 2, 2), (2, 2, 2, 1), (1, 2, 2, 2), (0, 0, 2, 2), (1, 1, 2, 2))
PART_SLOT = ((1, 4, 1, 2), (1, 0, 1, 5), (6, 0, 0, 0), (3, 3, 0, 0), (3, 3, 0, 0))
SENT = ((1, 1, 1, 1), (1, 0, 1, 1), (1, 0, 1, 1), (2, 2, 1, 0), (3, 3, 0, 0))


def normalize(embed):
    wide = embed.astype(jnp.float32)
    inverse = lax.rsqrt(jnp.sum(wide * wide, axis=1, keepdims=True) + 1e-06)
    return wide * inverse, inverse


def finish(embed, back):
    unit, inverse = normalize(embed)
    return inverse * (back - unit * jnp.sum(unit * back, axis=1, keepdims=True))


def encode(value):
    top = jnp.max(jnp.abs(value), axis=1, keepdims=True)
    step = (jnp.maximum(top, 1e-30) * (1.008 / 16383.0)).astype(jnp.bfloat16).astype(jnp.float32)
    scaled = value * ((1.0 / 128.0) / step)
    upper = jnp.floor(scaled)
    power = ((scaled - upper) * 128.0 + (ROUND - 71.0)) - ROUND
    signed = upper + jnp.where(upper >= 0.0, 128.0, -127.0)
    return (signed * jnp.exp2(power)).astype(jnp.bfloat16), step.astype(jnp.bfloat16)


def decode(code, step):
    wide = code.astype(jnp.float32)
    power = jnp.floor(jnp.log2(jnp.abs(wide)) + 0.001)
    upper = wide * jnp.exp2(14.0 - power) + jnp.where(wide >= 0.0, -16320.0, 16320.0)
    return (upper + power) * step.astype(jnp.float32)


def dot(a, b, dims):
    return lax.dot_general(a, b, dims, preferred_element_type=jnp.float32)


def kernel(
    n_blk, n_grp,
    scale_ref, bias_ref, image_hbm, text_hbm,
    grad_image_ref, grad_text_ref, sums_ref,
    image_ref, text_ref, load_sem, images, texts, own_text, scores, weights, parts, wires, inbox, late_wires,
    image_part, image_other, core_in, back_wires, relay, image_in, acc, totals,
    ring_send, ring_recv, share_send, share_recv, first_send, hand_send, text_recv,
    part_send, late_send, part_recv, core_send, core_recv, back_send, relay_recv, image_recv,
    total_send, total_recv,
):
    rows, width = image_ref.shape
    chunk = rows // 2
    p = lax.axis_index("blk")
    g = lax.axis_index("grp")
    c = lax.rem(p, 2)
    z = p // 4
    low = lax.rem(p // 2, 2)
    h = g // 4
    y = lax.rem(g, 4)
    x = 2 * h + low
    role = lax.rem(x + 4 - 2 * c, 4)
    depth = n_blk // 4

    def place(dz, dx, core):
        at_x = lax.rem(x + dx + 4, 4)
        at_z = lax.rem(z + dz + depth, depth)
        return (at_z * 4 + lax.rem(at_x, 2) * 2 + core, (at_x // 2) * 4 + y)

    def along_y(d):
        return (p, h * 4 + lax.rem(y + d + 4, 4))

    sibling = (p + 1 - 2 * c, g)

    def pick(row):
        a, b, d, e = row
        return jnp.where(role == 0, a, jnp.where(role == 1, b, jnp.where(role == 2, d, e)))

    def look(table, i):
        value = jnp.int32(0)
        for k, row in enumerate(table):
            value = jnp.where(i == k, pick(row), value)
        return value

    def half(ref, k):
        return ref.at[pl.ds(k * chunk, chunk)]

    def remote(src, dst, send, recv, device):
        return pltpu.make_async_remote_copy(
            src_ref=src, dst_ref=dst, send_sem=send, recv_sem=recv, device_id=device, device_id_type=MESH
        )

    rounds = (8, 4, depth)
    seats = (2 * y + c, x, z)

    def peer(r, d):
        seat = lax.rem(seats[r] + d, rounds[r])
        if r == 0:
            return (p - c + lax.rem(seat, 2), h * 4 + seat // 2)
        if r == 1:
            return (z * 4 + lax.rem(seat, 2) * 2 + c, (seat // 2) * 4 + y)
        return (seat * 4 + lax.rem(p, 4), g)

    image_load = pltpu.make_async_copy(image_hbm, image_ref, load_sem.at[0])
    text_load = pltpu.make_async_copy(text_hbm, text_ref, load_sem.at[1])
    image_load.start()
    text_load.start()

    barrier = pltpu.get_barrier_semaphore()
    greeted = [along_y(1), along_y(-1)]
    greeted += [place(dz, dx, core) for dz, dx in ((0, 1), (0, -1), (1, 0), (-1, 0)) for core in (0, 1)]
    greeted += [peer(r, d) for r in range(3) for d in range(1, rounds[r])]
    for device in greeted:
        pl.semaphore_signal(barrier, inc=1, device_id=device, device_id_type=MESH)

    image_load.wait()
    images[c, 0] = normalize(image_ref[...])[0].astype(jnp.bfloat16)
    text_load.wait()
    own_text[...] = normalize(text_ref[...])[0].astype(jnp.bfloat16)

    parts[pl.ds(5, 2)] = jnp.zeros((2, rows, width), jnp.float32)
    acc[...] = jnp.zeros_like(acc)

    pl.semaphore_wait(barrier, len(greeted))

    def ring(k):
        slot, part, to, into = ((0, 0, 1, 3), (0, 1, -1, 1), (0, 1, 1, 3), (0, 0, -1, 1), (3, 0, 1, 2), (1, 1, -1, 2))[k]
        return remote(
            half(images.at[c, slot], part), half(images.at[c, into], part),
            ring_send.at[k], ring_recv.at[into, part], along_y(to),
        )

    def ring_arrival(slot, part):
        remote(
            half(images.at[c, slot], part), half(images.at[c, slot], part),
            ring_send.at[0], ring_recv.at[slot, part], sibling,
        ).wait_recv()

    def share(slot):
        return remote(images.at[c, slot], images.at[c, slot], share_send.at[slot], share_recv.at[slot], sibling)

    far = low == 1
    first_hops = (
        (place(0, 0, h), 3 + c, c != h),
        (place(0, jnp.where(far & (c == 1), -1, 1), h), jnp.where(far, 5, 1 + c), None),
        (place(jnp.where(far, 1, 0), jnp.where(far, 0, -1), h), jnp.where(far, jnp.where(c == 0, 5, 0), 1 + c), None),
        (place(1, 0, h), 0, jnp.logical_not(far) & (c == 1)),
    )

    def first(k, part):
        device, into, _ = first_hops[k]
        return remote(
            half(own_text, part), half(texts.at[into], part), first_send.at[k, part], text_recv.at[into, part], device
        )

    hands = (
        (pick((5, 2, 5, 1)), place(0, pick((-1, 1, 1, -1)), c), pick((4, 4, 3, 3))),
        (pick((5, 5, 5, 4)), place(pick((1, 0, 1, 1)), pick((0, -1, 0, 0)), c), pick((2, 1, 1, 0))),
        (pick((0, 0, 4, 4)), place(pick((0, 0, 1, 1)), pick((0, 1, 0, 0)), c), pick((2, 2, 0, 0))),
    )

    def hand(k, part):
        slot, device, into = hands[k]
        return remote(
            half(texts.at[slot], part), half(texts.at[into], part), hand_send.at[k, part], text_recv.at[into, part], device
        )

    def text_arrival(slot, part):
        remote(
            half(own_text, part), half(texts.at[slot], part), first_send.at[0, 0], text_recv.at[slot, part], sibling
        ).wait_recv()

    def when(condition, action):
        if condition is None:
            action()
        else:
            pl.when(condition)(action)

    for part in range(2):
        ring(2 * part).start()
        ring(2 * part + 1).start()
        for k in (1, 2, 3, 0):
            when(first_hops[k][2], lambda k=k, part=part: first(k, part).start())
    share(0).start()

    @pl.when(c == h)
    def _():
        texts[3 + c] = own_text[...]


    for part in range(2):
        text_arrival(hands[0][0], part)
        hand(0, part).start()

        @pl.when(role == 1)
        def _():
            text_arrival(5, part)

        @pl.when(role < 3)
        def _():
            hand(1, part).start()

        @pl.when(role == 1)
        def _():
            text_arrival(0, part)
            hand(2, part).start()

        if part == 0:
            ring_arrival(3, 0)
            ring(4).start()
            ring_arrival(1, 1)
            ring(5).start()

    ring_arrival(3, 1)
    share(3).start()
    ring_arrival(1, 0)
    share(1).start()
    for part in range(2):

        @pl.when(role >= 2)
        def _():
            text_arrival(4, part)

        @pl.when(role == 2)
        def _():
            hand(2, part).start()

        @pl.when(role == 3)
        def _():
            hand(1, part).start()

    ring_arrival(2, 0)
    ring_arrival(2, 1)
    share(2).start()
    for slot in (0, 1, 3, 2):
        remote(
            images.at[c, slot], images.at[1 - c, slot], share_send.at[slot], share_recv.at[slot], sibling
        ).wait_recv()

    scale = jnp.exp(scale_ref[0])
    offset = bias_ref[0]
    strip = 32
    line = lax.broadcasted_iota(jnp.int32, (strip, rows), 0)
    column = lax.broadcasted_iota(jnp.int32, (strip, rows), 1)

    def fold(values):
        return values.reshape(-1, 8, rows).sum(axis=0)

    def tile(s, lane, into, paired, sums):
        losses, scales, biases = sums
        for k in range(rows // strip):
            lines = pl.ds(k * strip, strip)
            logits = scores[lines, pl.ds(lane, rows)]
            score = scale * logits + offset
            if paired is not None:
                match = (line + k * strip == column) & paired
                score = jnp.where(match, -score, score)
            small = jnp.exp(-jnp.abs(score))
            whole = 1.0 + small
            inverse = 1.0 / whole
            loss = jnp.maximum(score, 0.0) + (jnp.log(whole) + (small - (whole - 1.0)) * inverse)
            slope = jnp.where(score >= 0.0, 1.0, small) * inverse
            if paired is not None:
                slope = jnp.where(match, -slope, slope)
            weights[s, lines, into] = (scale * slope).astype(jnp.bfloat16)
            losses += fold(loss)
            scales += fold(slope * logits)
            biases += fold(slope)
        return losses, scales, biases

    def pairs_of(s, block, tiles, first_lane, paired):
        scores[:, pl.ds(0, tiles * rows)] = dot(texts[s], block, NT)
        sums = (acc[0], acc[1], acc[2])
        for t in range(tiles):
            if isinstance(first_lane, int):
                into = pl.ds(first_lane + t * rows, rows)
            else:
                into = pl.ds(pl.multiple_of(first_lane + t * rows, rows), rows)
            sums = tile(s, t * rows, into, paired if t == 0 else None, sums)
        acc[0], acc[1], acc[2] = sums
        if isinstance(first_lane, int):
            used = weights[s, :, pl.ds(first_lane, tiles * rows)]
        else:
            used = weights[s, :, pl.ds(pl.multiple_of(first_lane, tiles * rows), tiles * rows)]
        parts[s] = dot(used, block, NN)

    strip_rows = 32

    def lines_of(part, i):
        return pl.ds(pl.multiple_of(part * chunk + i * strip_rows, strip_rows), strip_rows)

    def strips(action):
        def body(i, carry):
            action(i)
            return carry

        lax.fori_loop(0, chunk // strip_rows, body, 0, unroll=2)

    def pack(value, wire, into):
        code, step = encode(value)
        wire[into + (pl.ds(0, width),)] = code
        wire[into + (pl.ds(width, 128),)] = jnp.broadcast_to(step, (strip_rows, 128))

    def unpack(wire, at):
        return decode(wire[at + (pl.ds(0, width),)], wire[at + (pl.ds(width, 128),)][:, 0:1])

    def part_copy(i, part):
        core = look(PART_CORE, i)
        device = place(look(PART_Z, i), look(PART_X, i), jnp.where(core == 2, c, core))
        s, into = look(ORDER, i), look(PART_SLOT, i)
        return remote(
            half(wires.at[s], part), half(inbox.at[into], part), part_send.at[i, part], part_recv.at[into, part], device
        )

    def part_sent(i):
        kind = look(SENT, i)
        return (kind == 1) | ((kind == 2) & (c == 1)) | ((kind == 3) & (c == 0))

    def text_step(i, carry):
        s = look(ORDER, i)
        sent = part_sent(i)

        @pl.when(sent)
        def _():
            text_arrival(s, 0)
            text_arrival(s, 1)

        middle = (s > 0) & (s < 4)

        @pl.when(middle)
        def _():
            pairs_of(s, images[...].reshape(8 * rows, width), 8, 0, (c == h) & (s == 3))

        @pl.when(jnp.logical_not(middle))
        def _():
            b = jnp.where(s == 4, 1, 0)
            pairs_of(s, images[b].reshape(4 * rows, width), 4, b * 4 * rows, (c == h) & (s == 4))

        @pl.when(sent)
        def _():
            for part in range(2):

                def code(k):
                    lines = lines_of(part, k)
                    pack(parts[s, lines], wires, (s, lines))

                strips(code)
                part_copy(i, part).start()

        return carry

    lax.fori_loop(0, 5, text_step, 0)

    def total_copy(r, d):
        seat = seats[r]
        return remote(
            totals.at[r, seat], totals.at[r, seat], total_send.at[r, d - 1], total_recv.at[r, seat], peer(r, d)
        )

    def total_sum(r):
        for d in range(1, rounds[r]):
            seat = lax.rem(seats[r] + d, rounds[r])
            remote(
                totals.at[r, seat], totals.at[r, seat], total_send.at[r, d - 1], total_recv.at[r, seat], sibling
            ).wait_recv()
        value = totals[r, 0]
        for seat in range(1, rounds[r]):
            value += totals[r, seat]
        return value

    def total_start(r, value):
        totals[r, seats[r]] = value
        for d in range(1, rounds[r]):
            total_copy(r, d).start()

    total_start(0, jnp.concatenate([jnp.sum(acc[k], axis=0, keepdims=True)[None] for k in range(3)], axis=0))

    def image_sum(b, slot):
        lanes = pl.ds(pl.multiple_of((4 * b + slot) * rows, rows), rows)
        lhs = weights[pl.ds(b, 4), :, lanes].reshape(4 * rows, rows)
        rhs = texts[pl.ds(b, 4)].reshape(4 * rows, width)
        return dot(lhs, rhs, TN)

    def core_copy(slot):
        return remote(image_other.at[slot], core_in.at[slot], core_send.at[slot], core_recv.at[slot], sibling)

    def other_step(i, carry):
        slot = jnp.where(i < 2, 2 + i, 3 - i)
        image_other[slot] = image_sum(1 - c, slot)
        core_copy(slot).start()
        return carry

    lax.fori_loop(0, 4, other_step, 0)

    def own_step(i, carry):
        slot = jnp.where(i < 2, 2 + i, 3 - i)
        image_part[slot] = image_sum(c, slot)
        return carry

    lax.fori_loop(0, 4, own_step, 0)
    total_start(1, total_sum(0))

    def back(k):
        slot, part, to, dst, sem = (
            (2, 0, 1, half(relay, 0), relay_recv.at[0]),
            (2, 1, -1, half(relay, 1), relay_recv.at[1]),
            (1, 1, 1, half(image_in.at[0], 1), image_recv.at[0, 1]),
            (3, 0, -1, half(image_in.at[1], 0), image_recv.at[1, 0]),
            (1, 0, 1, half(image_in.at[0], 0), image_recv.at[0, 0]),
            (3, 1, -1, half(image_in.at[1], 1), image_recv.at[1, 1]),
        )[k]
        return remote(half(back_wires.at[slot], part), dst, back_send.at[k], sem, along_y(to))

    def back_start(k, slot, part, add=None):
        def code(i):
            lines = lines_of(part, i)
            value = image_part[slot, lines]
            if add is not None:
                value += unpack(add, (lines,))
            pack(value, back_wires, (slot, lines))

        strips(code)
        back(k).start()

    for slot, ready in ((2, ((0, 0), (1, 1))), (3, ((3, 0),)), (1, ((2, 1),)), (0, ())):
        core_copy(slot).wait_recv()
        image_part[slot] += core_in[slot]
        for k, part in ready:
            back_start(k, slot, part)

    lates = (
        (pick((5, 0, 4, 4)), 0, place(pick((0, -1, 0, 0)), pick((1, 0, -1, 1)), jnp.where(role < 2, 1, c)), pick((4, 5, 2, 0))),
        (pick((5, 5, 5, 1)), pick((1, 1, 2, 1)), place(pick((0, -1, 0, 0)), pick((0, 0, -1, 1)), 0), pick((5, 5, 4, 5))),
        (2, 2, place(0, -1, 1), 4),
    )
    late_on = (None, role > 0, role == 1)

    def late(k, part):
        _, _, device, into = lates[k]
        return remote(
            half(late_wires.at[k], part), half(inbox.at[into], part), late_send.at[k, part], part_recv.at[into, part], device
        )

    def part_arrival(slot, part):
        remote(
            half(inbox.at[slot], part), half(inbox.at[slot], part), late_send.at[0, 0], part_recv.at[slot, part], sibling
        ).wait_recv()

    def absorb(into, slot, part):
        def add(i):
            lines = lines_of(part, i)
            parts[into, lines] += unpack(inbox, (slot, lines))

        strips(add)

    def late_start(k, part):
        into, slot, _, _ = lates[k]

        def add(i):
            lines = lines_of(part, i)
            pack(parts[into, lines] + unpack(inbox, (slot, lines)), late_wires, (k, lines))

        strips(add)
        late(k, part).start()

    def late_0(part):
        @pl.when(role == 0)
        def _():
            part_arrival(1, part)
            absorb(5, 1, part)

        part_arrival(0, part)
        late_start(0, part)

    def late_1(part):
        part_arrival(1, part)

        @pl.when(role == 2)
        def _():
            absorb(5, 1, part)
            part_arrival(2, part)

        late_start(1, part)

    def late_2(part):
        part_arrival(2, part)
        late_start(2, part)

    def relayed(k):
        slot, part = ((1, 0), (3, 1))[k]
        remote(half(relay, k), half(relay, k), back_send.at[0], relay_recv.at[k], sibling).wait_recv()
        back_start(4 + k, slot, part, relay)

    pl.when(role == 1)(lambda: late_1(0))
    pl.when(role > 1)(lambda: late_0(0))
    pl.when(role == 1)(lambda: late_1(1))
    pl.when(role > 1)(lambda: late_0(1))
    total_start(2, total_sum(1))
    pl.when(role == 1)(lambda: late_0(0))
    pl.when(role > 1)(lambda: late_1(0))
    relayed(0)
    relayed(1)
    pl.when(role == 1)(lambda: late_0(1))
    pl.when(role > 1)(lambda: late_1(1))
    pl.when(role == 0)(lambda: late_0(0))
    pl.when(role == 1)(lambda: late_2(0))
    pl.when(role == 0)(lambda: late_0(1))
    pl.when(role == 1)(lambda: late_2(1))
    total = jnp.sum(total_sum(2), axis=-1, keepdims=True)
    pairs = float(n_blk * n_grp * rows * STEPS * n_grp * rows)
    sums_ref[0:1, :] = jnp.broadcast_to(total[0] / pairs, (1, 128))
    sums_ref[1:2, :] = jnp.broadcast_to(total[1] * scale / pairs, (1, 128))
    sums_ref[2:3, :] = jnp.broadcast_to(total[2] / pairs, (1, 128))

    for part in range(2):
        for slot in range(2):
            remote(
                half(image_in.at[slot], part), half(image_in.at[slot], part),
                back_send.at[0], image_recv.at[slot, part], sibling,
            ).wait_recv()

        def last(i):
            lines = lines_of(part, i)
            total = image_part[0, lines] + unpack(image_in, (0, lines)) + unpack(image_in, (1, lines))
            grad_image_ref[lines] = finish(image_ref[lines], total)

        strips(last)

    extra = jnp.logical_not(far) & (c == 1)
    own = jnp.where(c == h, 3 + c, 6)
    for part in range(2):

        @pl.when(c != h)
        def _():
            part_arrival(3, part)
            absorb(6, 3, part)

        part_arrival(4, part)

        @pl.when(extra)
        def _():
            part_arrival(6, part)
            absorb(own, 6, part)

        part_arrival(5, part)

        def last(i):
            lines = lines_of(part, i)
            total = parts[own, lines] + unpack(inbox, (4, lines)) + unpack(inbox, (5, lines))
            grad_text_ref[lines] = finish(text_ref[lines], total)

        strips(last)

    for k in range(6):
        ring(k).wait_send()
        back(k).wait_send()
    for slot in range(4):
        share(slot).wait_send()
        core_copy(slot).wait_send()
    for part in range(2):
        for k in range(4):
            when(first_hops[k][2], lambda k=k, part=part: first(k, part).wait_send())
        hand(0, part).wait_send()
        hand(1, part).wait_send()
        pl.when((role == 1) | (role == 2))(lambda part=part: hand(2, part).wait_send())
        for k in range(3):
            when(late_on[k], lambda k=k, part=part: late(k, part).wait_send())

    def drain(i, carry):
        @pl.when(part_sent(i))
        def _():
            part_copy(i, 0).wait_send()
            part_copy(i, 1).wait_send()

        return carry

    lax.fori_loop(0, 5, drain, 0)
    for r in range(3):
        for d in range(1, rounds[r]):
            total_copy(r, d).wait_send()


def local(n_blk, n_grp, image_embed, text_embed, log_scale, bias):
    rows, width = image_embed.shape
    low, wide = jnp.bfloat16, jnp.float32
    dma = pltpu.SemaphoreType.DMA
    vmem = pl.BlockSpec(memory_space=pltpu.VMEM)
    smem = pl.BlockSpec(memory_space=pltpu.SMEM)
    hbm = pl.BlockSpec(memory_space=pltpu.HBM)
    out = jax.ShapeDtypeStruct((rows, width), wide)
    pairs = n_grp * rows * STEPS * rows
    grad_image, grad_text, sums = pl.pallas_call(
        functools.partial(kernel, n_blk, n_grp),
        out_shape=(out, out, jax.ShapeDtypeStruct((8, 128), wide)),
        in_specs=[smem, smem, hbm, hbm],
        out_specs=(vmem, vmem, vmem),
        scratch_shapes=[
            pltpu.VMEM((rows, width), low),
            pltpu.VMEM((rows, width), low),
            dma((2,)),
            pltpu.VMEM((2, 4, rows, width), low),
            pltpu.VMEM((6, rows, width), low),
            pltpu.VMEM((rows, width), low),
            pltpu.VMEM((rows, 8 * rows), wide),
            pltpu.VMEM((5, rows, 8 * rows), low),
            pltpu.VMEM((7, rows, width), wide),
            pltpu.VMEM((5, rows, width + 128), low),
            pltpu.VMEM((7, rows, width + 128), low),
            pltpu.VMEM((3, rows, width + 128), low),
            pltpu.VMEM((4, rows, width), wide),
            pltpu.VMEM((4, rows, width), wide),
            pltpu.VMEM((4, rows, width), wide),
            pltpu.VMEM((4, rows, width + 128), low),
            pltpu.VMEM((rows, width + 128), low),
            pltpu.VMEM((2, rows, width + 128), low),
            pltpu.VMEM((3, 8, 128), wide),
            pltpu.VMEM((3, 8, 3, 1, 128), wide),
            dma((6,)), dma((4, 2)), dma((4,)), dma((4,)), dma((4, 2)), dma((3, 2)), dma((6, 2)),
            dma((5, 2)), dma((3, 2)), dma((7, 2)), dma((4,)), dma((4,)), dma((6,)), dma((2,)), dma((2, 2)),
            dma((3, 8)), dma((3, 8)),
        ],
        compiler_params=pltpu.CompilerParams(
            collective_id=0, has_side_effects=True, vmem_limit_bytes=48 << 20
        ),
        cost_estimate=pl.CostEstimate(
            flops=6 * pairs * width, bytes_accessed=12 * rows * width, transcendentals=3 * pairs
        ),
        name="pair_loss",
    )(
        log_scale, bias,
        pltpu.with_memory_space_constraint(image_embed, pltpu.HBM),
        pltpu.with_memory_space_constraint(text_embed, pltpu.HBM),
    )
    return grad_image, grad_text, sums[0, 0], sums[1, 0], sums[2, 0]


def solution(mesh):
    split = P(("blk", "grp"), None)
    return jax.shard_map(
        functools.partial(local, mesh.shape["blk"], mesh.shape["grp"]),
        mesh=mesh,
        in_specs=(split, split, P(), P()),
        out_specs=(split, split, P(), P(), P()),
        check_vma=False,
    )
```

```python
import functools

import jax
import jax.numpy as jnp
from jax import lax
from jax.experimental import pallas as pl
from jax.experimental.pallas import tpu as pltpu
from jax.sharding import PartitionSpec as P

MESH = pl.DeviceIdType.MESH
STEPS = 4
ROUND = 12582912.0
NT = (((1,), (1,)), ((), ()))
TN = (((0,), (0,)), ((), ()))
NN = (((1,), (0,)), ((), ()))

ORDER = ((2, 1, 1, 2), (1, 0, 3, 3), (0, 2, 2, 0), (3, 3, 0, 4), (4, 4, 4, 1))
PART_Z = ((-1, 0, -1, 0), (0, 0, 0, 0), (-1, 0, 0, -1), (0, 0, -1, 0), (0, 0, 0, 0))
PART_X = ((0, -1, 0, 1), (1, 0, 1, -1), (0, 0, -1, 0), (0, 0, 0, 0), (0, 0, 0, 0))
PART_CORE = ((2, 0, 2, 1), (2, 2, 2, 2), (1, 2, 2, 2), (0, 0, 2, 2), (1, 1, 2, 2))
PART_SLOT = ((1, 4, 1, 5), (1, 0, 1, 2), (6, 0, 0, 0), (3, 3, 0, 0), (3, 3, 0, 0))
SENT = ((1, 1, 1, 1), (1, 0, 1, 1), (1, 0, 1, 1), (2, 2, 1, 0), (3, 3, 0, 0))


def normalize(embed):
    wide = embed.astype(jnp.float32)
    inverse = lax.rsqrt(jnp.sum(wide * wide, axis=1, keepdims=True) + 1e-06)
    return wide * inverse, inverse


def finish(embed, back):
    unit, inverse = normalize(embed)
    return inverse * (back - unit * jnp.sum(unit * back, axis=1, keepdims=True))


def encode(value):
    top = jnp.max(jnp.abs(value), axis=1, keepdims=True)
    step = (jnp.maximum(top, 1e-30) * (1.008 / 16383.0)).astype(jnp.bfloat16).astype(jnp.float32)
    scaled = value * ((1.0 / 128.0) / step)
    upper = jnp.floor(scaled)
    power = ((scaled - upper) * 128.0 + (ROUND - 71.0)) - ROUND
    signed = upper + jnp.where(upper >= 0.0, 128.0, -127.0)
    return (signed * jnp.exp2(power)).astype(jnp.bfloat16), step.astype(jnp.bfloat16)


def decode(code, step):
    wide = code.astype(jnp.float32)
    power = jnp.floor(jnp.log2(jnp.abs(wide)) + 0.001)
    upper = wide * jnp.exp2(14.0 - power) + jnp.where(wide >= 0.0, -16320.0, 16320.0)
    return (upper + power) * step.astype(jnp.float32)


def dot(a, b, dims):
    return lax.dot_general(a, b, dims, preferred_element_type=jnp.float32)


def kernel(
    n_blk, n_grp,
    scale_ref, bias_ref, image_hbm, text_hbm,
    grad_image_ref, grad_text_ref, sums_ref,
    image_ref, text_ref, load_sem, images, texts, own_text, scores, weights, parts, wires, inbox, late_wires,
    image_part, image_other, core_in, back_wires, relay, image_in, acc, totals,
    ring_send, ring_recv, share_send, share_recv, first_send, hand_send, text_recv,
    part_send, late_send, part_recv, core_send, core_recv, back_send, relay_recv, image_recv,
    total_send, total_recv,
):
    rows, width = image_ref.shape
    chunk = rows // 2
    p = lax.axis_index("blk")
    g = lax.axis_index("grp")
    c = lax.rem(p, 2)
    z = p // 4
    low = lax.rem(p // 2, 2)
    h = g // 4
    y = lax.rem(g, 4)
    x = 2 * h + low
    role = lax.rem(x + 4 - 2 * c, 4)
    depth = n_blk // 4

    def place(dz, dx, core):
        at_x = lax.rem(x + dx + 4, 4)
        at_z = lax.rem(z + dz + depth, depth)
        return (at_z * 4 + lax.rem(at_x, 2) * 2 + core, (at_x // 2) * 4 + y)

    def along_y(d):
        return (p, h * 4 + lax.rem(y + d + 4, 4))

    sibling = (p + 1 - 2 * c, g)

    def pick(row):
        a, b, d, e = row
        return jnp.where(role == 0, a, jnp.where(role == 1, b, jnp.where(role == 2, d, e)))

    def look(table, i):
        value = jnp.int32(0)
        for k, row in enumerate(table):
            value = jnp.where(i == k, pick(row), value)
        return value

    def half(ref, k):
        return ref.at[pl.ds(k * chunk, chunk)]

    def remote(src, dst, send, recv, device):
        return pltpu.make_async_remote_copy(
            src_ref=src, dst_ref=dst, send_sem=send, recv_sem=recv, device_id=device, device_id_type=MESH
        )

    rounds = (8, 4, depth)
    seats = (2 * y + c, x, z)

    def peer(r, d):
        seat = lax.rem(seats[r] + d, rounds[r])
        if r == 0:
            return (p - c + lax.rem(seat, 2), h * 4 + seat // 2)
        if r == 1:
            return (z * 4 + lax.rem(seat, 2) * 2 + c, (seat // 2) * 4 + y)
        return (seat * 4 + lax.rem(p, 4), g)

    image_load = pltpu.make_async_copy(image_hbm, image_ref, load_sem.at[0])
    text_load = pltpu.make_async_copy(text_hbm, text_ref, load_sem.at[1])
    image_load.start()
    text_load.start()

    barrier = pltpu.get_barrier_semaphore()
    greeted = [along_y(1), along_y(-1)]
    greeted += [place(dz, dx, core) for dz, dx in ((0, 1), (0, -1), (1, 0), (-1, 0)) for core in (0, 1)]
    greeted += [peer(r, d) for r in range(3) for d in range(1, rounds[r])]
    for device in greeted:
        pl.semaphore_signal(barrier, inc=1, device_id=device, device_id_type=MESH)

    image_load.wait()
    images[c, 0] = normalize(image_ref[...])[0].astype(jnp.bfloat16)
    text_load.wait()
    own_text[...] = normalize(text_ref[...])[0].astype(jnp.bfloat16)

    parts[pl.ds(5, 2)] = jnp.zeros((2, rows, width), jnp.float32)
    acc[...] = jnp.zeros_like(acc)

    pl.semaphore_wait(barrier, len(greeted))

    def ring(k):
        slot, part, to, into = ((0, 0, 1, 3), (0, 1, -1, 1), (0, 1, 1, 3), (0, 0, -1, 1), (3, 0, 1, 2), (1, 1, -1, 2))[k]
        return remote(
            half(images.at[c, slot], part), half(images.at[c, into], part),
            ring_send.at[k], ring_recv.at[into, part], along_y(to),
        )

    def ring_arrival(slot, part):
        remote(
            half(images.at[c, slot], part), half(images.at[c, slot], part),
            ring_send.at[0], ring_recv.at[slot, part], sibling,
        ).wait_recv()

    def share(slot):
        return remote(images.at[c, slot], images.at[c, slot], share_send.at[slot], share_recv.at[slot], sibling)

    far = low == 1
    first_hops = (
        (place(0, 0, h), 3 + c, c != h),
        (place(0, jnp.where(far & (c == 1), -1, 1), h), jnp.where(far, 5, 1 + c), None),
        (place(jnp.where(far, 1, 0), jnp.where(far, 0, -1), h), jnp.where(far, jnp.where(c == 0, 5, 0), 1 + c), None),
        (place(1, 0, h), 0, jnp.logical_not(far) & (c == 1)),
    )

    def first(k, part):
        device, into, _ = first_hops[k]
        return remote(
            half(own_text, part), half(texts.at[into], part), first_send.at[k, part], text_recv.at[into, part], device
        )

    hands = (
        (pick((5, 2, 5, 1)), place(0, pick((-1, 1, 1, -1)), c), pick((4, 4, 3, 3))),
        (pick((5, 5, 5, 4)), place(pick((1, 0, 1, 1)), pick((0, -1, 0, 0)), c), pick((2, 1, 1, 0))),
        (pick((0, 0, 4, 4)), place(pick((0, 0, 1, 1)), pick((0, 1, 0, 0)), c), pick((2, 2, 0, 0))),
    )

    def hand(k, part):
        slot, device, into = hands[k]
        return remote(
            half(texts.at[slot], part), half(texts.at[into], part), hand_send.at[k, part], text_recv.at[into, part], device
        )

    def text_arrival(slot, part):
        remote(
            half(own_text, part), half(texts.at[slot], part), first_send.at[0, 0], text_recv.at[slot, part], sibling
        ).wait_recv()

    def when(condition, action):
        if condition is None:
            action()
        else:
            pl.when(condition)(action)

    for part in range(2):
        ring(2 * part).start()
        ring(2 * part + 1).start()
        for k in (1, 2, 3, 0):
            when(first_hops[k][2], lambda k=k, part=part: first(k, part).start())
    share(0).start()

    @pl.when(c == h)
    def _():
        texts[3 + c] = own_text[...]


    for part in range(2):
        text_arrival(hands[0][0], part)
        hand(0, part).start()

        @pl.when(role == 1)
        def _():
            text_arrival(5, part)

        @pl.when(role < 3)
        def _():
            hand(1, part).start()

        @pl.when(role == 1)
        def _():
            text_arrival(0, part)
            hand(2, part).start()

        if part == 0:
            ring_arrival(3, 0)
            ring(4).start()
            ring_arrival(1, 1)
            ring(5).start()

    ring_arrival(3, 1)
    share(3).start()
    ring_arrival(1, 0)
    share(1).start()
    for part in range(2):

        @pl.when(role >= 2)
        def _():
            text_arrival(4, part)

        @pl.when(role == 2)
        def _():
            hand(2, part).start()

        @pl.when(role == 3)
        def _():
            hand(1, part).start()

    ring_arrival(2, 0)
    ring_arrival(2, 1)
    share(2).start()
    for slot in (0, 1, 3, 2):
        remote(
            images.at[c, slot], images.at[1 - c, slot], share_send.at[slot], share_recv.at[slot], sibling
        ).wait_recv()

    scale = jnp.exp(scale_ref[0])
    offset = bias_ref[0]
    strip = 32
    line = lax.broadcasted_iota(jnp.int32, (strip, rows), 0)
    column = lax.broadcasted_iota(jnp.int32, (strip, rows), 1)

    def fold(values):
        return values.reshape(-1, 8, rows).sum(axis=0)

    def tile(s, lane, into, paired, sums):
        losses, scales, biases = sums
        for k in range(rows // strip):
            lines = pl.ds(k * strip, strip)
            logits = scores[lines, pl.ds(lane, rows)]
            score = scale * logits + offset
            if paired is not None:
                match = (line + k * strip == column) & paired
                score = jnp.where(match, -score, score)
            small = jnp.exp(-jnp.abs(score))
            whole = 1.0 + small
            inverse = 1.0 / whole
            loss = jnp.maximum(score, 0.0) + (jnp.log(whole) + (small - (whole - 1.0)) * inverse)
            slope = jnp.where(score >= 0.0, 1.0, small) * inverse
            if paired is not None:
                slope = jnp.where(match, -slope, slope)
            weights[s, lines, into] = (scale * slope).astype(jnp.bfloat16)
            losses += fold(loss)
            scales += fold(slope * logits)
            biases += fold(slope)
        return losses, scales, biases

    def pairs_of(s, block, tiles, first_lane, paired):
        scores[:, pl.ds(0, tiles * rows)] = dot(texts[s], block, NT)
        sums = (acc[0], acc[1], acc[2])
        for t in range(tiles):
            if isinstance(first_lane, int):
                into = pl.ds(first_lane + t * rows, rows)
            else:
                into = pl.ds(pl.multiple_of(first_lane + t * rows, rows), rows)
            sums = tile(s, t * rows, into, paired if t == 0 else None, sums)
        acc[0], acc[1], acc[2] = sums
        if isinstance(first_lane, int):
            used = weights[s, :, pl.ds(first_lane, tiles * rows)]
        else:
            used = weights[s, :, pl.ds(pl.multiple_of(first_lane, tiles * rows), tiles * rows)]
        parts[s] = dot(used, block, NN)

    strip_rows = 32

    def lines_of(part, i):
        return pl.ds(pl.multiple_of(part * chunk + i * strip_rows, strip_rows), strip_rows)

    def strips(action):
        def body(i, carry):
            action(i)
            return carry

        lax.fori_loop(0, chunk // strip_rows, body, 0, unroll=2)

    def pack(value, wire, into):
        code, step = encode(value)
        wire[into + (pl.ds(0, width),)] = code
        wire[into + (pl.ds(width, 128),)] = jnp.broadcast_to(step, (strip_rows, 128))

    def unpack(wire, at):
        return decode(wire[at + (pl.ds(0, width),)], wire[at + (pl.ds(width, 128),)][:, 0:1])

    def part_copy(i, part):
        core = look(PART_CORE, i)
        device = place(look(PART_Z, i), look(PART_X, i), jnp.where(core == 2, c, core))
        s, into = look(ORDER, i), look(PART_SLOT, i)
        return remote(
            half(wires.at[s], part), half(inbox.at[into], part), part_send.at[i, part], part_recv.at[into, part], device
        )

    def part_sent(i):
        kind = look(SENT, i)
        return (kind == 1) | ((kind == 2) & (c == 1)) | ((kind == 3) & (c == 0))

    def text_step(i, carry):
        s = look(ORDER, i)
        sent = part_sent(i)

        @pl.when(sent)
        def _():
            text_arrival(s, 0)
            text_arrival(s, 1)

        middle = (s > 0) & (s < 4)

        @pl.when(middle)
        def _():
            pairs_of(s, images[...].reshape(8 * rows, width), 8, 0, (c == h) & (s == 3))

        @pl.when(jnp.logical_not(middle))
        def _():
            b = jnp.where(s == 4, 1, 0)
            pairs_of(s, images[b].reshape(4 * rows, width), 4, b * 4 * rows, (c == h) & (s == 4))

        @pl.when(sent)
        def _():
            for part in range(2):

                def code(k):
                    lines = lines_of(part, k)
                    pack(parts[s, lines], wires, (s, lines))

                strips(code)
                part_copy(i, part).start()

        return carry

    lax.fori_loop(0, 5, text_step, 0)

    def total_copy(r, d):
        seat = seats[r]
        return remote(
            totals.at[r, seat], totals.at[r, seat], total_send.at[r, d - 1], total_recv.at[r, seat], peer(r, d)
        )

    def total_sum(r):
        for d in range(1, rounds[r]):
            seat = lax.rem(seats[r] + d, rounds[r])
            remote(
                totals.at[r, seat], totals.at[r, seat], total_send.at[r, d - 1], total_recv.at[r, seat], sibling
            ).wait_recv()
        value = totals[r, 0]
        for seat in range(1, rounds[r]):
            value += totals[r, seat]
        return value

    def total_start(r, value):
        totals[r, seats[r]] = value
        for d in range(1, rounds[r]):
            total_copy(r, d).start()

    total_start(0, jnp.concatenate([jnp.sum(acc[k], axis=0, keepdims=True)[None] for k in range(3)], axis=0))

    def image_sum(b, slot):
        lanes = pl.ds(pl.multiple_of((4 * b + slot) * rows, rows), rows)
        lhs = weights[pl.ds(b, 4), :, lanes].reshape(4 * rows, rows)
        rhs = texts[pl.ds(b, 4)].reshape(4 * rows, width)
        return dot(lhs, rhs, TN)

    def core_copy(slot):
        return remote(image_other.at[slot], core_in.at[slot], core_send.at[slot], core_recv.at[slot], sibling)

    def other_step(i, carry):
        slot = jnp.where(i < 2, 2 + i, 3 - i)
        image_other[slot] = image_sum(1 - c, slot)
        core_copy(slot).start()
        return carry

    lax.fori_loop(0, 4, other_step, 0)

    def own_step(i, carry):
        slot = jnp.where(i < 2, 2 + i, 3 - i)
        image_part[slot] = image_sum(c, slot)
        return carry

    lax.fori_loop(0, 4, own_step, 0)
    total_start(1, total_sum(0))

    def back(k):
        slot, part, to, dst, sem = (
            (2, 0, 1, half(relay, 0), relay_recv.at[0]),
            (2, 1, -1, half(relay, 1), relay_recv.at[1]),
            (1, 1, 1, half(image_in.at[0], 1), image_recv.at[0, 1]),
            (3, 0, -1, half(image_in.at[1], 0), image_recv.at[1, 0]),
            (1, 0, 1, half(image_in.at[0], 0), image_recv.at[0, 0]),
            (3, 1, -1, half(image_in.at[1], 1), image_recv.at[1, 1]),
        )[k]
        return remote(half(back_wires.at[slot], part), dst, back_send.at[k], sem, along_y(to))

    def back_start(k, slot, part, add=None):
        def code(i):
            lines = lines_of(part, i)
            value = image_part[slot, lines]
            if add is not None:
                value += unpack(add, (lines,))
            pack(value, back_wires, (slot, lines))

        strips(code)
        back(k).start()

    for slot, ready in ((2, ((0, 0), (1, 1))), (3, ((3, 0),)), (1, ((2, 1),)), (0, ())):
        core_copy(slot).wait_recv()
        image_part[slot] += core_in[slot]
        for k, part in ready:
            back_start(k, slot, part)

    lates = (
        (pick((5, 0, 4, 4)), 0, place(pick((0, -1, 0, 0)), pick((1, 0, -1, 1)), jnp.where(role < 2, 1, c)), pick((4, 5, 2, 0))),
        (pick((5, 5, 5, 1)), pick((1, 1, 2, 1)), place(pick((0, -1, 0, 0)), pick((0, 0, -1, 1)), 0), pick((5, 5, 4, 5))),
        (2, 2, place(0, -1, 1), 4),
    )
    late_on = (None, role > 0, role == 1)

    def late(k, part):
        _, _, device, into = lates[k]
        return remote(
            half(late_wires.at[k], part), half(inbox.at[into], part), late_send.at[k, part], part_recv.at[into, part], device
        )

    def part_arrival(slot, part):
        remote(
            half(inbox.at[slot], part), half(inbox.at[slot], part), late_send.at[0, 0], part_recv.at[slot, part], sibling
        ).wait_recv()

    def absorb(into, slot, part):
        def add(i):
            lines = lines_of(part, i)
            parts[into, lines] += unpack(inbox, (slot, lines))

        strips(add)

    def late_start(k, part):
        into, slot, _, _ = lates[k]

        def add(i):
            lines = lines_of(part, i)
            pack(parts[into, lines] + unpack(inbox, (slot, lines)), late_wires, (k, lines))

        strips(add)
        late(k, part).start()

    def late_0(part):
        @pl.when(role == 0)
        def _():
            part_arrival(1, part)
            absorb(5, 1, part)

        part_arrival(0, part)
        late_start(0, part)

    def late_1(part):
        part_arrival(1, part)

        @pl.when(role == 2)
        def _():
            absorb(5, 1, part)
            part_arrival(2, part)

        late_start(1, part)

    def late_2(part):
        part_arrival(2, part)
        late_start(2, part)

    def relayed(k):
        slot, part = ((1, 0), (3, 1))[k]
        remote(half(relay, k), half(relay, k), back_send.at[0], relay_recv.at[k], sibling).wait_recv()
        back_start(4 + k, slot, part, relay)

    pl.when(role == 1)(lambda: late_1(0))
    pl.when(role > 1)(lambda: late_0(0))
    pl.when(role == 1)(lambda: late_1(1))
    pl.when(role > 1)(lambda: late_0(1))
    total_start(2, total_sum(1))
    pl.when(role == 1)(lambda: late_0(0))
    pl.when(role > 1)(lambda: late_1(0))
    relayed(0)
    relayed(1)
    pl.when(role == 1)(lambda: late_0(1))
    pl.when(role > 1)(lambda: late_1(1))
    pl.when(role == 0)(lambda: late_0(0))
    pl.when(role == 1)(lambda: late_2(0))
    pl.when(role == 0)(lambda: late_0(1))
    pl.when(role == 1)(lambda: late_2(1))
    total = jnp.sum(total_sum(2), axis=-1, keepdims=True)
    pairs = float(n_blk * n_grp * rows * STEPS * n_grp * rows)
    sums_ref[0:1, :] = jnp.broadcast_to(total[0] / pairs, (1, 128))
    sums_ref[1:2, :] = jnp.broadcast_to(total[1] * scale / pairs, (1, 128))
    sums_ref[2:3, :] = jnp.broadcast_to(total[2] / pairs, (1, 128))

    for part in range(2):
        for slot in range(2):
            remote(
                half(image_in.at[slot], part), half(image_in.at[slot], part),
                back_send.at[0], image_recv.at[slot, part], sibling,
            ).wait_recv()

        def last(i):
            lines = lines_of(part, i)
            total = image_part[0, lines] + unpack(image_in, (0, lines)) + unpack(image_in, (1, lines))
            grad_image_ref[lines] = finish(image_ref[lines], total)

        strips(last)

    extra = jnp.logical_not(far) & (c == 1)
    own = jnp.where(c == h, 3 + c, 6)
    for part in range(2):

        @pl.when(c != h)
        def _():
            part_arrival(3, part)
            absorb(6, 3, part)

        part_arrival(4, part)

        @pl.when(extra)
        def _():
            part_arrival(6, part)
            absorb(own, 6, part)

        part_arrival(5, part)

        def last(i):
            lines = lines_of(part, i)
            total = parts[own, lines] + unpack(inbox, (4, lines)) + unpack(inbox, (5, lines))
            grad_text_ref[lines] = finish(text_ref[lines], total)

        strips(last)

    for k in range(6):
        ring(k).wait_send()
        back(k).wait_send()
    for slot in range(4):
        share(slot).wait_send()
        core_copy(slot).wait_send()
    for part in range(2):
        for k in range(4):
            when(first_hops[k][2], lambda k=k, part=part: first(k, part).wait_send())
        hand(0, part).wait_send()
        hand(1, part).wait_send()
        pl.when((role == 1) | (role == 2))(lambda part=part: hand(2, part).wait_send())
        for k in range(3):
            when(late_on[k], lambda k=k, part=part: late(k, part).wait_send())

    def drain(i, carry):
        @pl.when(part_sent(i))
        def _():
            part_copy(i, 0).wait_send()
            part_copy(i, 1).wait_send()

        return carry

    lax.fori_loop(0, 5, drain, 0)
    for r in range(3):
        for d in range(1, rounds[r]):
            total_copy(r, d).wait_send()


def local(n_blk, n_grp, image_embed, text_embed, log_scale, bias):
    rows, width = image_embed.shape
    low, wide = jnp.bfloat16, jnp.float32
    dma = pltpu.SemaphoreType.DMA
    vmem = pl.BlockSpec(memory_space=pltpu.VMEM)
    smem = pl.BlockSpec(memory_space=pltpu.SMEM)
    hbm = pl.BlockSpec(memory_space=pltpu.HBM)
    out = jax.ShapeDtypeStruct((rows, width), wide)
    pairs = n_grp * rows * STEPS * rows
    grad_image, grad_text, sums = pl.pallas_call(
        functools.partial(kernel, n_blk, n_grp),
        out_shape=(out, out, jax.ShapeDtypeStruct((8, 128), wide)),
        in_specs=[smem, smem, hbm, hbm],
        out_specs=(vmem, vmem, vmem),
        scratch_shapes=[
            pltpu.VMEM((rows, width), low),
            pltpu.VMEM((rows, width), low),
            dma((2,)),
            pltpu.VMEM((2, 4, rows, width), low),
            pltpu.VMEM((6, rows, width), low),
            pltpu.VMEM((rows, width), low),
            pltpu.VMEM((rows, 8 * rows), wide),
            pltpu.VMEM((5, rows, 8 * rows), low),
            pltpu.VMEM((7, rows, width), wide),
            pltpu.VMEM((5, rows, width + 128), low),
            pltpu.VMEM((7, rows, width + 128), low),
            pltpu.VMEM((3, rows, width + 128), low),
            pltpu.VMEM((4, rows, width), wide),
            pltpu.VMEM((4, rows, width), wide),
            pltpu.VMEM((4, rows, width), wide),
            pltpu.VMEM((4, rows, width + 128), low),
            pltpu.VMEM((rows, width + 128), low),
            pltpu.VMEM((2, rows, width + 128), low),
            pltpu.VMEM((3, 8, 128), wide),
            pltpu.VMEM((3, 8, 3, 1, 128), wide),
            dma((6,)), dma((4, 2)), dma((4,)), dma((4,)), dma((4, 2)), dma((3, 2)), dma((6, 2)),
            dma((5, 2)), dma((3, 2)), dma((7, 2)), dma((4,)), dma((4,)), dma((6,)), dma((2,)), dma((2, 2)),
            dma((3, 8)), dma((3, 8)),
        ],
        compiler_params=pltpu.CompilerParams(
            collective_id=0, has_side_effects=True, vmem_limit_bytes=48 << 20
        ),
        cost_estimate=pl.CostEstimate(
            flops=6 * pairs * width, bytes_accessed=12 * rows * width, transcendentals=3 * pairs
        ),
        name="pair_loss",
    )(
        log_scale, bias,
        pltpu.with_memory_space_constraint(image_embed, pltpu.HBM),
        pltpu.with_memory_space_constraint(text_embed, pltpu.HBM),
    )
    return grad_image, grad_text, sums[0, 0], sums[1, 0], sums[2, 0]


def solution(mesh):
    split = P(("blk", "grp"), None)
    return jax.shard_map(
        functools.partial(local, mesh.shape["blk"], mesh.shape["grp"]),
        mesh=mesh,
        in_specs=(split, split, P(), P()),
        out_specs=(split, split, P(), P(), P()),
        check_vma=False,
    )
```
